256 devices in a mesh: dp: 16 (over z_hi, y), space: 16 (over z_lo, x, core).
Axes of the slice: x: 4, y: 4, z: 8 (z_hi: 4, z_lo: 2; z = z_hi * 2 + z_lo), core: 2. Of those that a mesh axis runs over, the one named last changes fastest.
Arguments:
- feature_maps: bfloat16 [16, 48, 48, 2048], P('dp', 'space'), may hold values from -12 to 12
- w_atrous: bfloat16 [3, 9, 2048, 256], P(None, None, 'space'), may hold values from -0.046875 to 0.046875
- w_point: bfloat16 [2048, 256], P('space'), may hold values from -0.125 to 0.125
- w_pool: bfloat16 [2048, 256], P('space'), may hold values from -0.125 to 0.125
- bias_branch: float32 [5, 256], P(None, 'space'), may hold values from -4 to 4
- w_proj: bfloat16 [5, 256, 256], P(None, 'space'), may hold values from -0.15625 to 0.15625
- bias_proj: float32 [256], replicated, may hold values from -4 to 4
- cotangent: bfloat16 [16, 48, 48, 256], P('dp', 'space'), may hold values from -6 to 6
Outputs:
- head_out: bfloat16 [16, 48, 48, 256], P('dp', 'space')
- grad_maps: bfloat16 [16, 48, 48, 2048], P('dp', 'space')
- grad_atrous: float32 [3, 9, 2048, 256], P(None, None, 'space')
- grad_point: float32 [2048, 256], P('space')
- grad_pool: float32 [2048, 256], P('space')
- grad_bias: float32 [5, 256], P(None, 'space')
- grad_proj: float32 [5, 256, 256], P(None, 'space')
- grad_proj_bias: float32 [256], replicated
The draws below stay inside these ranges and needn't reach their ends.
All inputs are finite; a program needn't handle non-finite values.
Results may differ from the reference program's by a relative error of at most 0.029.
Values may be sent and summed in bfloat16 or wider, within the bound.
A program may use at most 192 MiB of HBM per device.

```python
import jax
import jax.numpy as jnp
from jax import lax

CHANNELS = 2048
BRANCH_CH = 256
HEIGHT = 48
WIDTH = 48
SAMPLES = 16


def draw_feature_maps(key, part):
    key = jax.random.fold_in(key, 7)
    noise_key, offset_key = jax.random.split(key, 2)
    full_shape = (SAMPLES, HEIGHT, WIDTH, CHANNELS)
    offsets = jax.random.normal(offset_key, (SAMPLES, 1, 1, CHANNELS), jnp.float32)
    texture = jax.random.normal(noise_key, full_shape, jnp.float32)
    return jnp.clip(texture + offsets, -12.0, 12.0).astype(jnp.bfloat16)


def block_scale(stream_key, extent, cuts, smallest, high):
    def one(axis_at, shards_of):
        draws = jax.random.uniform(jax.random.fold_in(jax.random.fold_in(stream_key, 6), axis_at), (shards_of,), jnp.float32, smallest / len(cuts), high / len(cuts))
        return jnp.repeat(jnp.exp(draws), extent[axis_at] // shards_of).reshape((-1,) + (1,) * (len(extent) - axis_at - 1))

    level = one(*cuts[0])
    for cut in cuts[1:]:
        level = level * one(*cut)
    return level


def scatter_about(key, extent, scale, limit, shards=(), kind=jnp.bfloat16):
    values = jax.random.normal(key, extent, jnp.float32) * scale
    if len(shards) > 0:
        values = block_scale(key, extent, shards, -0.22, 0.18) * values
    return jnp.clip(values, min=-limit, max=limit).astype(kind)


def setup_inputs(seed: int = 0) -> dict:
    key_list = jax.random.split(jax.random.key(seed), 9)
    feature_maps = draw_feature_maps(jax.random.fold_in(key_list[8], 71), 0)
    w_atrous = scatter_about(key_list[1], (3, 9, CHANNELS, BRANCH_CH), (9 * CHANNELS) ** -0.5, 0.046875, ((2, 16),))
    w_point = scatter_about(key_list[2], (CHANNELS, BRANCH_CH), CHANNELS ** -0.5, 0.125, ((0, 16),))
    w_pool = scatter_about(key_list[3], (CHANNELS, BRANCH_CH), CHANNELS ** -0.5, 0.125, ((0, 16),))
    bias_branch = scatter_about(key_list[4], (5, BRANCH_CH), 1.0, 4.0, ((1, 16),), jnp.float32)
    w_proj = scatter_about(key_list[5], (5, BRANCH_CH, BRANCH_CH), (5 * BRANCH_CH) ** -0.5, 0.15625, ((1, 16),))
    bias_proj = scatter_about(key_list[6], (BRANCH_CH,), 1.0, 4.0, (), jnp.float32)
    cotangent = scatter_about(key_list[7], (SAMPLES, HEIGHT, WIDTH, BRANCH_CH), 1.0, 6.0, ((0, 16), (1, 16)))
    return {"feature_maps": feature_maps, "w_atrous": w_atrous, "w_point": w_point, "w_pool": w_pool, "bias_branch": bias_branch, "w_proj": w_proj, "bias_proj": bias_proj, "cotangent": cotangent}


dilations = (6, 12, 18)
margin_cells = 18


def silu_slope(values):
    sigma = jax.nn.sigmoid(values)
    return sigma * (1.0 + values * (1.0 - sigma))


def tap_stack(planes, dilation):
    height = planes.shape[0]
    columns = planes.shape[1]
    padded = jnp.pad(planes, ((margin_cells, margin_cells), (margin_cells, margin_cells), (0, 0)))
    pieces = []
    for row_tap in range(3):
        for col_tap in range(3):
            row_start = margin_cells + (row_tap - 1) * dilation
            col_start = margin_cells + (col_tap - 1) * dilation
            pieces.append(padded[row_start:row_start + height, col_start:col_start + columns])
    return jnp.concatenate(pieces, axis=-1)


def reference(feature_maps, w_atrous, w_point, w_pool, bias_branch, w_proj, bias_proj, cotangent):
    pixels = HEIGHT * WIDTH
    proj_flat = w_proj.reshape(5 * BRANCH_CH, BRANCH_CH)

    def per_sample(running, inputs):
        planes, cotan = inputs
        flattened = planes.reshape(pixels, CHANNELS)
        responses = []
        for branch_no in range(3):
            taps = tap_stack(planes, dilations[branch_no]).reshape(pixels, 9 * CHANNELS)
            weights = w_atrous[branch_no].reshape(9 * CHANNELS, BRANCH_CH)
            responses.append(jnp.dot(taps, weights, preferred_element_type=jnp.float32))
        responses.append(jnp.dot(flattened, w_point, preferred_element_type=jnp.float32))
        branch_pre = jnp.stack(responses, axis=1) + bias_branch[:4][None]
        pooled = (jnp.sum(flattened, axis=0, dtype=jnp.float32) / pixels).astype(jnp.bfloat16)
        pool_pre = jnp.dot(pooled[None], w_pool, preferred_element_type=jnp.float32)[0] + bias_branch[4]
        activated = jax.nn.silu(branch_pre).astype(jnp.bfloat16)
        pool_act = jax.nn.silu(pool_pre).astype(jnp.bfloat16)
        joined = jnp.concatenate([activated, jnp.broadcast_to(pool_act[None, None], (pixels, 1, BRANCH_CH))], axis=1)
        joined = joined.reshape(pixels, 5 * BRANCH_CH)
        head_pre = jnp.dot(joined, proj_flat, preferred_element_type=jnp.float32) + bias_proj
        head_out = jax.nn.silu(head_pre).astype(jnp.bfloat16)
        grad_out = (cotan.reshape(pixels, BRANCH_CH).astype(jnp.float32) * silu_slope(head_pre)).astype(jnp.bfloat16)
        grad_proj_bias = jnp.sum(grad_out, axis=0, dtype=jnp.float32)
        grad_proj = jnp.dot(joined.T, grad_out, preferred_element_type=jnp.float32).reshape(5, BRANCH_CH, BRANCH_CH)
        grad_act = jnp.dot(grad_out, proj_flat.T, preferred_element_type=jnp.float32).reshape(pixels, 5, BRANCH_CH)
        grad_pre = (grad_act[:, :4] * silu_slope(branch_pre)).astype(jnp.bfloat16)
        grad_pool_pre = (silu_slope(pool_pre) * jnp.sum(grad_act[:, 4], axis=0)).astype(jnp.bfloat16)
        pool_term = grad_pool_pre.astype(jnp.float32)
        grad_bias = jnp.concatenate([jnp.sum(grad_pre, axis=0, dtype=jnp.float32), pool_term[None]], axis=0)
        grad_pool = pooled.astype(jnp.float32)[:, None] * pool_term[None]
        grad_point = jnp.dot(flattened.T, grad_pre[:, 3], preferred_element_type=jnp.float32)
        pool_back = jnp.dot(w_pool.astype(jnp.float32), pool_term, precision=lax.Precision.HIGHEST) / pixels
        grad_input = jnp.dot(grad_pre[:, 3], w_point.T, preferred_element_type=jnp.float32) + pool_back[None]
        tap_grads = []
        for branch_no in range(3):
            dilation = dilations[branch_no]
            taps = tap_stack(planes, dilation).reshape(pixels, 9 * CHANNELS)
            tap_grads.append(jnp.dot(taps.T, grad_pre[:, branch_no], preferred_element_type=jnp.float32).reshape(9, CHANNELS, BRANCH_CH))
            spread = tap_stack(grad_pre[:, branch_no].reshape(HEIGHT, WIDTH, BRANCH_CH), -dilation).reshape(pixels, 9 * BRANCH_CH)
            weights = jnp.transpose(w_atrous[branch_no], (0, 2, 1)).reshape(9 * BRANCH_CH, CHANNELS)
            grad_input = grad_input + jnp.dot(spread, weights, preferred_element_type=jnp.float32)
        grad_atrous = jnp.stack(tap_grads)
        totals = (running[0] + grad_atrous, running[1] + grad_point, running[2] + grad_pool,
                  running[3] + grad_bias, running[4] + grad_proj, running[5] + grad_proj_bias)
        outputs = (head_out.reshape(HEIGHT, WIDTH, BRANCH_CH),
                   grad_input.astype(jnp.bfloat16).reshape(HEIGHT, WIDTH, CHANNELS))
        return totals, outputs

    initial = (jnp.zeros((3, 9, CHANNELS, BRANCH_CH), jnp.float32), jnp.zeros((CHANNELS, BRANCH_CH), jnp.float32),
               jnp.zeros((CHANNELS, BRANCH_CH), jnp.float32), jnp.zeros((5, BRANCH_CH), jnp.float32),
               jnp.zeros((5, BRANCH_CH, BRANCH_CH), jnp.float32), jnp.zeros((BRANCH_CH,), jnp.float32))
    totals, outputs = lax.scan(per_sample, initial, (feature_maps, cotangent))
    return (outputs[0], outputs[1], totals[0], totals[1], totals[2], totals[3], totals[4], totals[5])
```

```python
import jax
import jax.numpy as jnp
from jax import lax
from jax.experimental import pallas as pl
from jax.experimental.pallas import tpu as pltpu
from jax.sharding import PartitionSpec as P

bf16 = jnp.bfloat16
f32 = jnp.float32
dilations = (6, 12, 18)
MESH = pl.DeviceIdType.MESH
ROWS = 144
PIX = 2304
PAD = 864
NT = (((1,), (1,)), ((), ()))
TN = (((0,), (0,)), ((), ()))
BLOCK = 576
VMEM_LIMIT = 60 * 2**20


def silu_slope(values):
    sigma = jax.nn.sigmoid(values)
    return sigma * (1.0 + values * (1.0 - sigma))


def dot(a, b):
    return jnp.dot(a, b, preferred_element_type=f32)


def dot_nt(a, b):
    return lax.dot_general(a, b, NT, preferred_element_type=f32)


def aligned(value, step=16):
    return value if isinstance(value, int) else pl.multiple_of(value, step)


class Links:
    def __init__(self, dp, space):
        self.dp = dp
        self.space = space
        self.sent = []

    def copy(self, src, dst, ssem, rsem, dp, space):
        return pltpu.make_async_remote_copy(
            src_ref=src, dst_ref=dst, send_sem=ssem, recv_sem=rsem, device_id=(dp, space), device_id_type=MESH
        )

    def send(self, src, dst, ssem, rsem, dp=None, space=None):
        c = self.copy(src, dst, ssem, rsem, self.dp if dp is None else dp, self.space if space is None else space)
        c.start()
        self.sent.append(c)

    def arrived(self, ref, rsem):
        self.copy(ref, ref, rsem, rsem, self.dp, self.space).wait_recv()

    def flush(self):
        for c in self.sent:
            c.wait_send()


def shifted(block, d, rows, sign):
    lanes = block.shape[1]
    v = block.reshape(rows, 48, lanes)
    col = lax.broadcasted_iota(jnp.int32, (rows, 48, lanes), 1)
    if sign < 0:
        v = jnp.where(col >= d, pltpu.roll(v, d, 1), 0.0)
    else:
        v = jnp.where(col < 48 - d, pltpu.roll(v, 48 - d, 1), 0.0)
    return v.reshape(rows * 48, lanes)


def forward_kernel(
    maps, w, w_point, w_pool, small, w_proj, bias_proj, cot,
    head_out, grad_pre, x_out, g_proj, sums, pool_out, pooled_out,
    x, c, part, core_out, core_in, acc, sa, sb, ra, rb, s2p, s2m, r2p, r2m, sz, rz, wp, msg, msgs,
    x_s, x_r, wp_s, wp_r, msg_s, msg_r, rs_s, rs_r,
):
    dp = lax.axis_index("dp")
    s = lax.axis_index("space")
    core = s % 2
    cx = (s // 2) % 4
    cz = s // 8
    xp = (cx + 1) % 4
    xm = (cx + 3) % 4
    x2 = (cx + 2) % 4
    right = (cz * 4 + xp) * 2 + core
    left = (cz * 4 + xm) * 2 + core
    other_z = ((1 - cz) * 4 + cx) * 2 + core
    sibling = (cz * 4 + cx) * 2 + 1 - core
    links = Links(dp, s)

    barrier = pltpu.get_barrier_semaphore()

    @pl.loop(1, 16)
    def _(o):
        pl.semaphore_signal(barrier, inc=1, device_id=(dp, (s + o) % 16), device_id_type=MESH)

    pl.semaphore_wait(barrier, 15)

    def map_copy(o):
        t = (s + o) % 16
        return links.copy(
            maps.at[:, pl.ds(aligned(t * 128, 128), 128)], x.at[pl.ds(aligned(s * ROWS), ROWS)],
            x_s.at[o], x_r.at[o], dp, t,
        )

    def proj_copy(o):
        part_rows = wp.at[:, pl.ds(aligned(s * 16), 16)]
        return links.copy(w_proj, part_rows, wp_s.at[o], wp_r.at[o], dp, (s + o) % 16)

    def msg_copy(o):
        return links.copy(msg, msgs.at[s], msg_s.at[o], msg_r.at[o], dp, (s + o) % 16)

    @pl.loop(1, 16)
    def _(o):
        map_copy(o).start()

    @pl.loop(1, 16)
    def _(o):
        proj_copy(o).start()

    x[pl.ds(aligned(s * ROWS), ROWS)] = maps[:, pl.ds(aligned(s * 128, 128), 128)]
    wp[:, pl.ds(aligned(s * 16), 16)] = w_proj[...]
    for k in range(3):
        c[k, 0:PAD] = jnp.zeros((PAD, 384), bf16)
        c[k, PAD + PIX : PAD + PIX + PAD] = jnp.zeros((PAD, 384), bf16)

    def build(o, total):
        t = (s + 16 - o) % 16
        at = aligned(t * ROWS)
        raw = x[pl.ds(at, ROWS)]
        v = raw.astype(f32)
        for k, d in enumerate(dilations):
            lo = shifted(v, d, 3, -1).astype(bf16)
            hi = shifted(v, d, 3, 1).astype(bf16)
            c[k, pl.ds(aligned(PAD + at), ROWS)] = jnp.concatenate([lo, raw, hi], axis=1)
        return total + jnp.sum(v.reshape(18, 8, 128), axis=0)

    total = build(0, jnp.zeros((8, 128), f32))

    def build_remote(o, total):
        t = (s + 16 - o) % 16
        links.arrived(x.at[pl.ds(aligned(t * ROWS), ROWS)], x_r.at[o])
        return build(o, total)

    total = lax.fori_loop(1, 16, build_remote, total)
    x_out[...] = x[...]

    pooled = (jnp.sum(total, axis=0, keepdims=True) / PIX).astype(bf16)
    pooled = jnp.broadcast_to(pooled, (16, 128))
    pooled_out[...] = pooled.astype(f32)[0:8]
    pool_part = dot(pooled, w_pool[...])[0:8]
    row = lax.broadcasted_iota(jnp.int32, (8, 256), 0)
    msg[...] = small[...] + jnp.where(row == 0, pool_part, 0.0)
    msgs[pl.ds(s, 1)] = msg[...][None]

    @pl.loop(1, 16)
    def _(o):
        msg_copy(o).start()

    def respond(k):
        @pl.loop(0, PIX // BLOCK)
        def _(i):
            at = aligned(i * BLOCK)
            if k < 3:
                d = dilations[k] * 48
                lhs = jnp.concatenate(
                    [c[k, pl.ds(aligned(PAD + at + (a - 1) * d), BLOCK)] for a in range(3)], axis=1
                )
                p = dot(lhs, w[k])
            else:
                p = dot(c[0, pl.ds(aligned(PAD + at), BLOCK), 128:256], w_point[...])
            part[k, pl.ds(i * (BLOCK // ROWS), BLOCK // ROWS)] = p.reshape(BLOCK // ROWS, ROWS, 256)

        @pl.loop(0, 8)
        def _(j):
            core_out[k, j] = part[k, 2 * j + 1 - core].astype(bf16)

        links.send(core_out.at[k], core_in.at[k], rs_s.at[k, 0], rs_r.at[k, 0], space=sibling)

    def step1(k):
        links.arrived(core_in.at[k], rs_r.at[k, 0])

        @pl.loop(0, 8)
        def _(j):
            acc[k, j] = part[k, 2 * j + core] + core_in[k, j].astype(f32)

        sa[k] = acc[k, x2].astype(bf16)
        links.send(sa.at[k], ra.at[k], rs_s.at[k, 1], rs_r.at[k, 1], space=right)
        sb[k] = acc[k, 4 + x2].astype(bf16)
        links.send(sb.at[k], rb.at[k], rs_s.at[k, 2], rs_r.at[k, 2], space=left)

    def step2(k):
        links.arrived(ra.at[k], rs_r.at[k, 1])
        s2p[k, 0] = (acc[k, xp] + ra[k].astype(f32)).astype(bf16)
        s2p[k, 1] = acc[k, 4 + xp].astype(bf16)
        links.send(s2p.at[k], r2p.at[k], rs_s.at[k, 3], rs_r.at[k, 3], space=right)
        links.arrived(rb.at[k], rs_r.at[k, 2])
        s2m[k, 0] = acc[k, xm].astype(bf16)
        s2m[k, 1] = (acc[k, 4 + xm] + rb[k].astype(f32)).astype(bf16)
        links.send(s2m.at[k], r2m.at[k], rs_s.at[k, 4], rs_r.at[k, 4], space=left)

    def step3(k):
        links.arrived(r2p.at[k], rs_r.at[k, 3])
        links.arrived(r2m.at[k], rs_r.at[k, 4])
        for z in range(2):
            acc[k, z * 4 + cx] = acc[k, z * 4 + cx] + (r2p[k, z].astype(f32) + r2m[k, z].astype(f32))
        sz[k] = acc[k, (1 - cz) * 4 + cx].astype(bf16)
        links.send(sz.at[k], rz.at[k], rs_s.at[k, 5], rs_r.at[k, 5], space=other_z)

    def step4(k):
        links.arrived(rz.at[k], rs_r.at[k, 5])
        return acc[k, cz * 4 + cx] + rz[k].astype(f32)

    respond(0)
    step1(0)
    respond(1)
    step1(1)
    step2(0)
    respond(2)
    step1(2)
    step2(1)
    step3(0)
    respond(3)
    step1(3)
    step2(2)
    step3(1)
    step2(3)

    @pl.loop(1, 16)
    def _(o):
        t = (s + 16 - o) % 16
        links.arrived(msgs.at[t], msg_r.at[o])
        links.arrived(wp.at[:, pl.ds(aligned(t * 16), 16)], wp_r.at[o])

    head_msg = lax.fori_loop(0, 16, lambda i, v: v + msgs[i], jnp.zeros((8, 256), f32))
    pool_pre = head_msg[0:1] + head_msg[5:6]
    pool_out[...] = jnp.broadcast_to(pool_pre, (8, 256))
    pool_act = jnp.broadcast_to(jax.nn.silu(pool_pre).astype(bf16).astype(f32), (ROWS, 256)).astype(bf16)

    step3(2)
    step3(3)

    slopes = []
    acts = []
    for k in range(4):
        pre = step4(k) + head_msg[1 + k : 2 + k]
        sigma = jax.nn.sigmoid(pre)
        slopes.append(sigma * (1.0 + pre * (1.0 - sigma)))
        acts.append((pre * sigma).astype(bf16))
    acts.append(pool_act)
    head = bias_proj[...] + sum(dot(acts[k], wp[k]) for k in range(5))
    sigma = jax.nn.sigmoid(head)
    head_out[...] = (head * sigma).astype(bf16)
    grad_f = cot[...].astype(f32) * (sigma * (1.0 + head * (1.0 - sigma)))
    grad = grad_f.astype(bf16)
    lines = []
    for k in range(4):
        g = (dot_nt(grad, wp[k]) * slopes[k]).astype(bf16)
        grad_pre[k] = g
        lines.append(jnp.sum(g.astype(f32), axis=0, keepdims=True))
    lines.append(jnp.sum(dot_nt(grad, wp[4]), axis=0, keepdims=True))
    lines.append(jnp.sum(grad.astype(f32), axis=0, keepdims=True))
    for i in range(6):
        sums[i : i + 1] = lines[i]
    sums[6:8] = jnp.zeros((2, 256), f32)
    for k in range(5):
        g_proj[k] = lax.dot_general(acts[k], grad, TN, preferred_element_type=f32).astype(bf16)

    @pl.loop(1, 16)
    def _(o):
        map_copy(o).wait_send()
        proj_copy(o).wait_send()
        msg_copy(o).wait_send()

    links.flush()


HALVES = (144, 144, 144, 48)


def backward_kernel(
    x, grad_pre, w, w_point, w_pool, g_proj, sums, pool_pre, pooled,
    d0, d1, d2, d3, maps_out,
    gp, g3, xt, dw0, dw1, dw2, dw3, u1s0, u1s1, u1s2, u1s3, u1r0, u1r1, u1r2, u1r3,
    u2s0, u2s1, u2s2, u2s3, u2r0, u2r1, u2r2, u2r3, es0, es1, es2, es3, zr0, zr1, zr2, zr3,
    zt0, zt1, zt2, zt3, own, gpr, msgs, gx,
    ag_s, ag_r, ar_s, ar_r, gp_s, gp_r, msg_s, msg_r, gx_s, gx_r,
):
    dp = lax.axis_index("dp")
    s = lax.axis_index("space")
    core = s % 2
    cx = (s // 2) % 4
    cz = s // 8
    xp = (cx + 1) % 4
    xm = (cx + 3) % 4
    x2 = (cx + 2) % 4

    def at(z, col, half):
        return (z * 4 + col) * 2 + half

    right = at(cz, xp, core)
    left = at(cz, xm, core)
    other_z = at(1 - cz, cx, core)
    sibling = at(cz, cx, 1 - core)
    y = dp % 4
    hz = dp // 4
    yp = (y + 1) % 4
    ym = (y + 3) % 4
    y2 = (y + 2) % 4
    up = hz * 4 + yp
    down = hz * 4 + ym
    links = Links(dp, s)

    barrier = pltpu.get_barrier_semaphore()

    @pl.loop(1, 16)
    def _(o):
        pl.semaphore_signal(barrier, inc=1, device_id=(dp, (s + o) % 16), device_id_type=MESH)

    pl.semaphore_signal(barrier, inc=1, device_id=(up, s), device_id_type=MESH)
    pl.semaphore_signal(barrier, inc=1, device_id=(down, s), device_id_type=MESH)
    for o in range(1, 4):
        pl.semaphore_signal(barrier, inc=1, device_id=(((hz + o) % 4) * 4 + y, s), device_id_type=MESH)
    pl.semaphore_wait(barrier, 20)

    def block(k, n):
        if k < 3:
            return gp.at[k, pl.ds(aligned(PAD + n * ROWS), ROWS)]
        return g3.at[pl.ds(aligned(n * ROWS), ROWS)]

    def pass_on(k, n, slot, to):
        b = block(k, n)
        links.send(b, b, ag_s.at[k, slot], ag_r.at[k, n], space=to)

    def have(k, n):
        links.arrived(block(k, n), ag_r.at[k, n])

    def own_block(k):
        mine = grad_pre[k]
        if k < 3:
            gp[k, pl.ds(aligned(PAD + s * ROWS), ROWS)] = mine
        else:
            g3[pl.ds(aligned(s * ROWS), ROWS)] = mine
        pass_on(k, s, 0, other_z)
        pass_on(k, s, 1, right)
        pass_on(k, s, 2, left)
        pass_on(k, s, 3, sibling)

    def gather1(k):
        n = at(1 - cz, cx, core)
        have(k, n)
        pass_on(k, n, 4, right)
        pass_on(k, n, 5, left)
        pass_on(k, n, 6, sibling)

    def gather2(k):
        n = at(0, xm, core)
        have(k, n)
        pass_on(k, n, 7, right)
        pass_on(k, n, 8, sibling)
        n = at(1, xp, core)
        have(k, n)
        pass_on(k, n, 9, left)
        pass_on(k, n, 10, sibling)
        n = at(1, xm, core)
        have(k, n)
        pass_on(k, n, 11, sibling)
        n = at(0, xp, core)
        have(k, n)
        pass_on(k, n, 12, sibling)

    def gather3(k):
        for z in range(2):
            n = at(z, x2, core)
            have(k, n)
            pass_on(k, n, 13 + z, sibling)
        for z in range(2):
            for col in (cx, xp, xm, x2):
                have(k, at(z, col, 1 - core))

    for k in range(4):
        own_block(k)

    def proj_copy(o):
        t = (s + o) % 16
        return links.copy(
            g_proj.at[:, pl.ds(aligned(t * 16), 16)], gpr.at[s], gp_s.at[o], gp_r.at[o], dp, t
        )

    def msg_copy(o):
        return links.copy(sums, msgs.at[s], msg_s.at[o], msg_r.at[o], dp, (s + o) % 16)

    @pl.loop(1, 16)
    def _(o):
        msg_copy(o).start()

    for k in range(3):
        gp[k, 0:PAD] = jnp.zeros((PAD, 256), bf16)
        gp[k, PAD + PIX : PAD + PIX + PAD] = jnp.zeros((PAD, 256), bf16)
    msgs[pl.ds(s, 1)] = sums[...][None]
    gpr[pl.ds(s, 1)] = g_proj[:, pl.ds(aligned(s * 16), 16)][None]

    def turn(i):
        st = aligned(i * 384, 128)
        v = x[pl.ds(st, 384)].astype(f32)
        mid = jnp.transpose(v).astype(bf16)
        for k, d in enumerate(dilations):
            xt[k, 0:128, pl.ds(st, 384)] = jnp.transpose(shifted(v, d, 8, -1)).astype(bf16)
            xt[k, 128:256, pl.ds(st, 384)] = mid
            xt[k, 256:384, pl.ds(st, 384)] = jnp.transpose(shifted(v, d, 8, 1)).astype(bf16)

    @pl.loop(0, 2)
    def _(i):
        turn(i)

    gather1(0)
    gather1(1)

    @pl.loop(2, 4)
    def _(i):
        turn(i)

    gather2(0)
    gather1(2)

    @pl.loop(4, 6)
    def _(i):
        turn(i)

    gather2(1)
    gather1(3)

    @pl.loop(1, 16)
    def _(o):
        proj_copy(o).start()

    gather3(0)

    dws = (dw0, dw1, dw2, dw3)
    outs = (d0, d1, d2, d3)
    u1s, u1r = (u1s0, u1s1, u1s2, u1s3), (u1r0, u1r1, u1r2, u1r3)
    u2s, u2r = (u2s0, u2s1, u2s2, u2s3), (u2r0, u2r1, u2r2, u2r3)
    es, zr, zt = (es0, es1, es2, es3), (zr0, zr1, zr2, zr3), (zt0, zt1, zt2, zt3)

    def weight_grad(k):
        d = 48 * dilations[k]
        for a, (lo, hi) in enumerate(
            ((0, -((d - PIX) // 128) * 128), (0, PIX), (d // 128 * 128, PIX))
        ):
            g0 = PAD + lo - (a - 1) * d
            dws[k][384 * a : 384 * (a + 1)] = dot(xt[k, :, lo:hi], gp[k, g0 : g0 + hi - lo])

    def sum1(k):
        h = HALVES[k]
        dw = dws[k]
        u1s[k][0] = dw[pl.ds(aligned(y2 * 2 * h), h)].astype(bf16)
        links.send(u1s[k].at[0], u1r[k].at[0], ar_s.at[k, 0], ar_r.at[k, 0], dp=up)
        u1s[k][1] = dw[pl.ds(aligned(y2 * 2 * h + h), h)].astype(bf16)
        links.send(u1s[k].at[1], u1r[k].at[1], ar_s.at[k, 1], ar_r.at[k, 1], dp=down)

    def sum2(k):
        h = HALVES[k]
        dw = dws[k]
        links.arrived(u1r[k].at[0], ar_r.at[k, 0])
        u2s[k][0, 0] = (dw[pl.ds(aligned(yp * 2 * h), h)] + u1r[k][0].astype(f32)).astype(bf16)
        u2s[k][0, 1] = dw[pl.ds(aligned(yp * 2 * h + h), h)].astype(bf16)
        links.send(u2s[k].at[0], u2r[k].at[0], ar_s.at[k, 2], ar_r.at[k, 2], dp=up)
        links.arrived(u1r[k].at[1], ar_r.at[k, 1])
        u2s[k][1, 0] = dw[pl.ds(aligned(ym * 2 * h), h)].astype(bf16)
        u2s[k][1, 1] = (dw[pl.ds(aligned(ym * 2 * h + h), h)] + u1r[k][1].astype(f32)).astype(bf16)
        links.send(u2s[k].at[1], u2r[k].at[1], ar_s.at[k, 3], ar_r.at[k, 3], dp=down)

    def sum3(k):
        h = HALVES[k]
        dw = dws[k]
        links.arrived(u2r[k].at[0], ar_r.at[k, 2])
        links.arrived(u2r[k].at[1], ar_r.at[k, 3])
        for half in range(2):
            v = dw[pl.ds(aligned(y * 2 * h + half * h), h)] + (
                u2r[k][0, half].astype(f32) + u2r[k][1, half].astype(f32)
            )
            for lane in range(2):
                quarter = v[:, 128 * lane : 128 * (lane + 1)]
                own[k, 2 * half + lane, 0:h] = quarter
                es[k][2 * half + lane] = quarter.astype(bf16)
        for o in range(1, 4):
            q = (hz + o) % 4
            links.send(es[k].at[q], zr[k].at[o - 1], ar_s.at[k, 3 + o], ar_r.at[k, 3 + o], dp=q * 4 + y)

    def sum4(k):
        h = HALVES[k]
        v = own[k, hz, 0:h]
        for o in range(1, 4):
            links.arrived(zr[k].at[o - 1], ar_r.at[k, 3 + o])
            v = v + zr[k][o - 1].astype(f32)
        zt[k][hz] = v.astype(bf16)
        for o in range(1, 4):
            q = (hz + o) % 4
            links.send(zt[k].at[hz], zt[k].at[hz], ar_s.at[k, 6 + o], ar_r.at[k, 6 + o], dp=q * 4 + y)

    def chunk(k, n):
        h = HALVES[k]
        return outs[k].at[pl.ds(aligned(n * 2 * h), 2 * h)]

    def half_chunk(k, n, half):
        h = HALVES[k]
        return outs[k].at[pl.ds(aligned(n * 2 * h + half * h), h)]

    def sum5(k):
        h = HALVES[k]
        for o in range(1, 4):
            links.arrived(zt[k].at[(hz + 4 - o) % 4], ar_r.at[k, 6 + o])
        for half in range(2):
            outs[k][pl.ds(aligned(y * 2 * h + half * h), h)] = jnp.concatenate(
                [zt[k][2 * half], zt[k][2 * half + 1]], axis=1
            )
        mine = chunk(k, y)
        links.send(mine, mine, ar_s.at[k, 10], ar_r.at[k, 10], dp=up)
        links.send(mine, mine, ar_s.at[k, 11], ar_r.at[k, 11], dp=down)

    def sum6(k):
        links.arrived(chunk(k, ym), ar_r.at[k, 10])
        b = half_chunk(k, ym, 0)
        links.send(b, b, ar_s.at[k, 12], ar_r.at[k, 12], dp=up)
        links.arrived(chunk(k, yp), ar_r.at[k, 11])
        b = half_chunk(k, yp, 1)
        links.send(b, b, ar_s.at[k, 13], ar_r.at[k, 13], dp=down)

    def sum7(k):
        links.arrived(half_chunk(k, y2, 0), ar_r.at[k, 12])
        links.arrived(half_chunk(k, y2, 1), ar_r.at[k, 13])

    weight_grad(0)
    sum1(0)
    gather2(2)
    gather3(1)
    weight_grad(1)
    sum1(1)
    sum2(0)
    gather2(3)
    gather3(2)
    weight_grad(2)
    sum1(2)
    sum2(1)
    sum3(0)
    gather3(3)

    dw3[0:128] = dot(xt[0, 128:256, :], g3[...])

    @pl.loop(1, 16)
    def _(o):
        t = (s + 16 - o) % 16
        links.arrived(msgs.at[t], msg_r.at[o])
        links.arrived(gpr.at[t], gp_r.at[o])

    totals = lax.fori_loop(0, 16, lambda i, v: v + msgs[i], jnp.zeros((8, 256), f32))
    pool_grad = (silu_slope(pool_pre[0:1]) * totals[4:5]).astype(bf16)
    pool_row = pool_grad.astype(f32)
    column = jnp.transpose(jnp.broadcast_to(pooled[0:1], (128, 128)))
    dw3[128:256] = jnp.concatenate([column, column], axis=1) * pool_row
    dw3[256:336] = lax.fori_loop(
        0, 16, lambda i, v: v + gpr[i].astype(f32).reshape(80, 256), jnp.zeros((80, 256), f32)
    )
    dw3[336:384] = jnp.zeros((48, 256), f32)
    dw3[336:340] = totals[0:4]
    dw3[340:341] = pool_row
    dw3[341:342] = totals[5:6]
    sum1(3)

    back = dot_nt(jnp.broadcast_to(pool_row, (16, 256)).astype(bf16), w_pool[...])[0:1] / PIX

    def input_grad(i):
        st = i * BLOCK
        result = dot_nt(g3[st : st + BLOCK], w_point[...]) + back
        for k in range(3):
            d = 48 * dilations[k]
            sides = 0.0
            for a in range(3):
                g0 = PAD + st - (a - 1) * d
                g = gp[k, g0 : g0 + BLOCK]
                tap = 384 * a
                ends = jnp.concatenate([w[k, tap : tap + 128], w[k, tap + 256 : tap + 384]], axis=0)
                sides = sides + dot_nt(g, ends)
                result = result + dot_nt(g, w[k, tap + 128 : tap + 256])
            result = result + shifted(sides[:, 0:128], dilations[k], BLOCK // 48, 1)
            result = result + shifted(sides[:, 128:256], dilations[k], BLOCK // 48, -1)
        gx[st : st + BLOCK] = result.astype(bf16)
        for j in range(BLOCK // ROWS):
            n = i * (BLOCK // ROWS) + j

            @pl.when(s != n)
            def _():
                gx_copy(n).start()

    def gx_copy(n):
        return links.copy(
            gx.at[pl.ds(n * ROWS, ROWS)], maps_out.at[:, pl.ds(aligned(s * 128, 128), 128)],
            gx_s.at[n], gx_r.at[s], dp, n,
        )

    input_grad(0)
    sum2(2)
    sum3(1)
    sum4(0)
    sum2(3)
    input_grad(1)
    sum3(2)
    sum4(1)
    sum5(0)
    sum3(3)
    input_grad(2)
    sum4(2)
    sum5(1)
    sum6(0)
    sum4(3)
    input_grad(3)
    sum5(2)
    sum6(1)
    sum7(0)
    sum5(3)
    maps_out[:, pl.ds(aligned(s * 128, 128), 128)] = gx[pl.ds(aligned(s * ROWS), ROWS)]
    sum6(2)
    sum6(3)

    @pl.loop(1, 16)
    def _(o):
        t = (s + o) % 16
        links.arrived(maps_out.at[:, pl.ds(aligned(t * 128, 128), 128)], gx_r.at[t])
        proj_copy(o).wait_send()
        msg_copy(o).wait_send()
        links.copy(
            gx.at[pl.ds(0, ROWS)], gx.at[pl.ds(0, ROWS)], gx_s.at[t], gx_s.at[t], dp, t
        ).wait_send()

    sum7(1)
    sum7(2)
    sum7(3)
    links.flush()


def dma(*shape):
    return pltpu.SemaphoreType.DMA(shape)


def vm(dtype, *shape):
    return pltpu.VMEM(shape, dtype)


def body(feature_maps, w_atrous, w_point, w_pool, bias_branch, w_proj, bias_proj, cotangent):
    s = lax.axis_index("space")
    vmem = pl.BlockSpec(memory_space=pltpu.VMEM)
    maps = feature_maps.reshape(ROWS, 2048)
    w = w_atrous.reshape(3, 1152, 256)
    small = lax.dynamic_update_slice(jnp.zeros((8, 256), f32), bias_branch, (1, s * 16))
    cot = cotangent.reshape(ROWS, 256)
    shape = jax.ShapeDtypeStruct
    head_out, grad_pre, x, g_proj, sums, pool_pre, pooled = pl.pallas_call(
        forward_kernel,
        out_shape=(
            shape((ROWS, 256), bf16), shape((4, ROWS, 256), bf16), shape((PIX, 128), bf16),
            shape((5, 256, 256), bf16), shape((8, 256), f32), shape((8, 256), f32), shape((8, 128), f32),
        ),
        in_specs=[vmem] * 8,
        out_specs=[vmem] * 7,
        scratch_shapes=[
            vm(bf16, PIX, 128), vm(bf16, 3, PIX + 2 * PAD, 384), vm(f32, 4, 16, ROWS, 256),
            vm(bf16, 4, 8, ROWS, 256), vm(bf16, 4, 8, ROWS, 256), vm(f32, 4, 8, ROWS, 256),
            vm(bf16, 4, ROWS, 256), vm(bf16, 4, ROWS, 256), vm(bf16, 4, ROWS, 256), vm(bf16, 4, ROWS, 256),
            vm(bf16, 4, 2, ROWS, 256), vm(bf16, 4, 2, ROWS, 256),
            vm(bf16, 4, 2, ROWS, 256), vm(bf16, 4, 2, ROWS, 256),
            vm(bf16, 4, ROWS, 256), vm(bf16, 4, ROWS, 256), vm(bf16, 5, 256, 256),
            vm(f32, 8, 256), vm(f32, 16, 8, 256),
            dma(16), dma(16), dma(16), dma(16), dma(16), dma(16), dma(4, 6), dma(4, 6),
        ],
        compiler_params=pltpu.CompilerParams(
            collective_id=0, has_side_effects=True, vmem_limit_bytes=VMEM_LIMIT
        ),
        name="aspp_forward",
    )(maps, w, w_point, w_pool, small, w_proj, bias_proj.reshape(1, 256), cot)

    sizes = [8 * h for h in HALVES]
    d0, d1, d2, d3, grad_maps = pl.pallas_call(
        backward_kernel,
        out_shape=tuple(shape((n, 256), bf16) for n in sizes) + (shape((ROWS, 2048), bf16),),
        in_specs=[vmem] * 9,
        out_specs=[vmem] * 5,
        scratch_shapes=[
            vm(bf16, 3, PIX + 2 * PAD, 256), vm(bf16, PIX, 256), vm(bf16, 3, 384, PIX),
            *[vm(f32, n, 256) for n in sizes],
            *[vm(bf16, 2, h, 256) for h in HALVES], *[vm(bf16, 2, h, 256) for h in HALVES],
            *[vm(bf16, 2, 2, h, 256) for h in HALVES], *[vm(bf16, 2, 2, h, 256) for h in HALVES],
            *[vm(bf16, 4, h, 128) for h in HALVES], *[vm(bf16, 3, h, 128) for h in HALVES],
            *[vm(bf16, 4, h, 128) for h in HALVES],
            vm(f32, 4, 4, 144, 128), vm(bf16, 16, 5, 16, 256), vm(f32, 16, 8, 256), vm(bf16, PIX, 128),
            dma(4, 15), dma(4, 16), dma(4, 14), dma(4, 14),
            dma(16), dma(16), dma(16), dma(16), dma(16), dma(16),
        ],
        compiler_params=pltpu.CompilerParams(
            collective_id=1, has_side_effects=True, vmem_limit_bytes=VMEM_LIMIT
        ),
        name="aspp_backward",
    )(x, grad_pre, w, w_point, w_pool, g_proj, sums, pool_pre, pooled)

    grad_atrous = jnp.stack([d.reshape(9, 128, 256) for d in (d0, d1, d2)]).astype(f32)
    rest = d3.astype(f32)
    grad_bias = lax.dynamic_slice(rest[336:341], (0, s * 16), (5, 16))
    return (
        head_out.reshape(1, 3, 48, 256),
        grad_maps.reshape(1, 3, 48, 2048),
        grad_atrous,
        rest[0:128],
        rest[128:256],
        grad_bias,
        rest[256:336].reshape(5, 16, 256),
        rest[341],
    )


def solution(mesh):
    placed = (
        P("dp", "space", None, None),
        P(None, None, "space", None),
        P("space", None),
        P("space", None),
        P(None, "space"),
        P(None, "space", None),
        P(),
        P("dp", "space", None, None),
    )
    return jax.shard_map(
        body,
        mesh=mesh,
        in_specs=placed,
        out_specs=(
            P("dp", "space", None, None),
            P("dp", "space", None, None),
            P(None, None, "space", None),
            P("space", None),
            P("space", None),
            P(None, "space"),
            P(None, "space", None),
            P(),
        ),
        check_vma=False,
    )
```

```python
import jax
import jax.numpy as jnp
from jax import lax
from jax.experimental import pallas as pl
from jax.experimental.pallas import tpu as pltpu
from jax.sharding import PartitionSpec as P

bf16 = jnp.bfloat16
f32 = jnp.float32
dilations = (6, 12, 18)
MESH = pl.DeviceIdType.MESH
ROWS = 144
PIX = 2304
PAD = 864
NT = (((1,), (1,)), ((), ()))
TN = (((0,), (0,)), ((), ()))
BLOCK = 576
VMEM_LIMIT = 60 * 2**20


def silu_slope(values):
    sigma = jax.nn.sigmoid(values)
    return sigma * (1.0 + values * (1.0 - sigma))


def dot(a, b):
    return jnp.dot(a, b, preferred_element_type=f32)


def dot_nt(a, b):
    return lax.dot_general(a, b, NT, preferred_element_type=f32)


def aligned(value, step=16):
    return value if isinstance(value, int) else pl.multiple_of(value, step)


class Links:
    def __init__(self, dp, space):
        self.dp = dp
        self.space = space
        self.sent = []

    def copy(self, src, dst, ssem, rsem, dp, space):
        return pltpu.make_async_remote_copy(
            src_ref=src, dst_ref=dst, send_sem=ssem, recv_sem=rsem, device_id=(dp, space), device_id_type=MESH
        )

    def send(self, src, dst, ssem, rsem, dp=None, space=None):
        c = self.copy(src, dst, ssem, rsem, self.dp if dp is None else dp, self.space if space is None else space)
        c.start()
        self.sent.append(c)

    def arrived(self, ref, rsem):
        self.copy(ref, ref, rsem, rsem, self.dp, self.space).wait_recv()

    def flush(self):
        for c in self.sent:
            c.wait_send()


def shifted(block, d, rows, sign):
    lanes = block.shape[1]
    v = block.reshape(rows, 48, lanes)
    col = lax.broadcasted_iota(jnp.int32, (rows, 48, lanes), 1)
    if sign < 0:
        v = jnp.where(col >= d, pltpu.roll(v, d, 1), 0.0)
    else:
        v = jnp.where(col < 48 - d, pltpu.roll(v, 48 - d, 1), 0.0)
    return v.reshape(rows * 48, lanes)


HALVES = (144, 144, 144, 48)
SMALL_BLOCK = 288


def aspp_kernel(
    maps, w, w_point, w_pool, bias, w_proj, bias_proj, cot,
    head_out, d0, d1, d2, d3, maps_out,
    x, c, core_out, core_in, acc, sa, sb, ra, rb, s2p, s2m, r2p, r2m, sz, rz, wp, slopes, acts,
    gp, g3, xt, dw0, dw1, dw2, dw3, u1s0, u1s1, u1s2, u1s3, u1r0, u1r1, u1r2, u1r3,
    u2s0, u2s1, u2s2, u2s3, u2r0, u2r1, u2r2, u2r3, es0, es1, es2, es3, zr0, zr1, zr2, zr3,
    zt0, zt1, zt2, zt3, own, gpo, gpi, gps, gpr, note, note_in, note_sum, notes, gx,
    x_s, x_r, wp_s, wp_r, wf_s, wf_r, rs_s, rs_r,
    ag_s, ag_r, ar_s, ar_r, gp_s, gp_r, note_s, note_r, gx_s, gx_r,
):
    dp = lax.axis_index("dp")
    s = lax.axis_index("space")
    core = s % 2
    chip = s // 2
    cx = chip % 4
    cz = chip // 4
    xp = (cx + 1) % 4
    xm = (cx + 3) % 4
    x2 = (cx + 2) % 4

    def at(z, col, half):
        return (z * 4 + col) * 2 + half

    right = at(cz, xp, core)
    left = at(cz, xm, core)
    other_z = at(1 - cz, cx, core)
    sibling = at(cz, cx, 1 - core)
    y = dp % 4
    hz = dp // 4
    yp = (y + 1) % 4
    ym = (y + 3) % 4
    y2 = (y + 2) % 4
    up = hz * 4 + yp
    down = hz * 4 + ym
    links = Links(dp, s)

    barrier = pltpu.get_barrier_semaphore()

    @pl.loop(1, 16)
    def _(o):
        pl.semaphore_signal(barrier, inc=1, device_id=(dp, (s + o) % 16), device_id_type=MESH)

    pl.semaphore_signal(barrier, inc=1, device_id=(up, s), device_id_type=MESH)
    pl.semaphore_signal(barrier, inc=1, device_id=(down, s), device_id_type=MESH)
    for o in range(1, 4):
        pl.semaphore_signal(barrier, inc=1, device_id=(((hz + o) % 4) * 4 + y, s), device_id_type=MESH)
    pl.semaphore_wait(barrier, 20)

    def map_copy(o):
        t = (s + o) % 16
        return links.copy(
            maps.at[:, pl.ds(aligned(t * 128, 128), 128)], x.at[pl.ds(aligned(s * ROWS), ROWS)],
            x_s.at[o], x_r.at[o], dp, t,
        )

    @pl.loop(1, 16)
    def _(o):
        map_copy(o).start()

    x[pl.ds(aligned(s * ROWS), ROWS)] = maps[:, pl.ds(aligned(s * 128, 128), 128)]
    wp[:, pl.ds(aligned(s * 16), 16)] = w_proj[...]
    for k in range(3):
        c[k, 0:PAD] = jnp.zeros((PAD, 384), bf16)
        c[k, PAD + PIX : PAD + PIX + PAD] = jnp.zeros((PAD, 384), bf16)
        gp[k, 0:PAD] = jnp.zeros((PAD, 256), bf16)
        gp[k, PAD + PIX : PAD + PIX + PAD] = jnp.zeros((PAD, 256), bf16)

    def build(o, total):
        t = (s + 16 - o) % 16
        base = aligned(t * ROWS)
        raw = x[pl.ds(base, ROWS)]
        v = raw.astype(f32)
        for k, d in enumerate(dilations):
            lo = shifted(v, d, 3, -1).astype(bf16)
            hi = shifted(v, d, 3, 1).astype(bf16)
            c[k, pl.ds(aligned(PAD + base), ROWS)] = jnp.concatenate([lo, raw, hi], axis=1)
        return total + jnp.sum(v.reshape(18, 8, 128), axis=0)

    total = build(0, jnp.zeros((8, 128), f32))

    def build_remote(o, total):
        t = (s + 16 - o) % 16
        links.arrived(x.at[pl.ds(aligned(t * ROWS), ROWS)], x_r.at[o])
        return build(o, total)

    total = lax.fori_loop(1, 16, build_remote, total)

    def proj_part(t):
        return wp.at[:, pl.ds(aligned(t * 16), 16)]

    def proj_copy(o):
        t = ((chip + o) % 8) * 2 + core
        return links.copy(proj_part(s), proj_part(s), wp_s.at[o], wp_r.at[o], dp, t)

    def proj_forward(o):
        t = ((chip + 8 - o) % 8) * 2 + core
        return links.copy(proj_part(t), proj_part(t), wf_s.at[o], wf_r.at[o], dp, sibling)

    @pl.loop(1, 8)
    def _(o):
        proj_copy(o).start()

    proj_forward(0).start()

    def note_first(n):
        links.send(note.at[n], note_in.at[n], note_s.at[n, 8], note_r.at[n, 8], space=sibling)

    def note_copy(n, o):
        t = ((chip + o) % 8) * 2 + core
        return links.copy(note_sum.at[n], notes.at[n, chip], note_s.at[n, o], note_r.at[n, o], dp, t)

    def note_second(n):
        links.arrived(note_in.at[n], note_r.at[n, 8])
        note_sum[n] = note[n] + note_in[n]
        notes[n, pl.ds(chip, 1)] = note_sum[n][None]

        @pl.loop(1, 8)
        def _(o):
            note_copy(n, o).start()

    def note_total(n):
        @pl.loop(1, 8)
        def _(o):
            links.arrived(notes.at[n, (chip + 8 - o) % 8], note_r.at[n, o])

        return lax.fori_loop(0, 8, lambda i, v: v + notes[n, i], jnp.zeros((8, 256), f32))

    def respond(k, lo, hi):
        @pl.loop(lo, hi)
        def _(i):
            base = aligned(i * BLOCK)
            if k < 3:
                d = dilations[k] * 48
                lhs = jnp.concatenate(
                    [c[k, pl.ds(aligned(PAD + base + (a - 1) * d), BLOCK)] for a in range(3)], axis=1
                )
                p = dot(lhs, w[k])
            else:
                p = dot(c[0, pl.ds(aligned(PAD + base), BLOCK), 128:256], w_point[...])
            p = p.reshape(2, 2, ROWS, 256)
            first = core == 0
            acc[k, pl.ds(i * 2, 2)] = jnp.where(first, p[:, 0], p[:, 1])
            core_out[k, pl.ds(i * 2, 2)] = jnp.where(first, p[:, 1], p[:, 0]).astype(bf16)

        if hi == PIX // BLOCK:
            links.send(core_out.at[k], core_in.at[k], rs_s.at[k, 0], rs_r.at[k, 0], space=sibling)

    def step1(k):
        links.arrived(core_in.at[k], rs_r.at[k, 0])

        @pl.loop(0, 8)
        def _(j):
            acc[k, j] = acc[k, j] + core_in[k, j].astype(f32)

        sa[k] = acc[k, x2].astype(bf16)
        links.send(sa.at[k], ra.at[k], rs_s.at[k, 1], rs_r.at[k, 1], space=right)
        sb[k] = acc[k, 4 + x2].astype(bf16)
        links.send(sb.at[k], rb.at[k], rs_s.at[k, 2], rs_r.at[k, 2], space=left)

    def step2(k):
        links.arrived(ra.at[k], rs_r.at[k, 1])
        s2p[k, 0] = (acc[k, xp] + ra[k].astype(f32)).astype(bf16)
        s2p[k, 1] = acc[k, 4 + xp].astype(bf16)
        links.send(s2p.at[k], r2p.at[k], rs_s.at[k, 3], rs_r.at[k, 3], space=right)
        links.arrived(rb.at[k], rs_r.at[k, 2])
        s2m[k, 0] = acc[k, xm].astype(bf16)
        s2m[k, 1] = (acc[k, 4 + xm] + rb[k].astype(f32)).astype(bf16)
        links.send(s2m.at[k], r2m.at[k], rs_s.at[k, 4], rs_r.at[k, 4], space=left)

    def step3(k):
        links.arrived(r2p.at[k], rs_r.at[k, 3])
        links.arrived(r2m.at[k], rs_r.at[k, 4])
        for z in range(2):
            acc[k, z * 4 + cx] = acc[k, z * 4 + cx] + (r2p[k, z].astype(f32) + r2m[k, z].astype(f32))
        sz[k] = acc[k, (1 - cz) * 4 + cx].astype(bf16)
        links.send(sz.at[k], rz.at[k], rs_s.at[k, 5], rs_r.at[k, 5], space=other_z)

    def step4(k):
        links.arrived(rz.at[k], rs_r.at[k, 5])
        return acc[k, cz * 4 + cx] + rz[k].astype(f32)

    def turn(lo, hi):
        @pl.loop(lo, hi)
        def _(i):
            st = aligned(i * 384, 128)
            v = x[pl.ds(st, 384)].astype(f32)
            mid = jnp.transpose(v).astype(bf16)
            for k, d in enumerate(dilations):
                xt[k, 0:128, pl.ds(st, 384)] = jnp.transpose(shifted(v, d, 8, -1)).astype(bf16)
                xt[k, 128:256, pl.ds(st, 384)] = mid
                xt[k, 256:384, pl.ds(st, 384)] = jnp.transpose(shifted(v, d, 8, 1)).astype(bf16)

    respond(3, 0, 4)

    pooled = (jnp.sum(total, axis=0, keepdims=True) / PIX).astype(bf16)
    pooled = jnp.broadcast_to(pooled, (16, 128))
    pool_part = dot(pooled, w_pool[...])[0:8]
    note[0] = jnp.zeros((8, 256), f32)
    for i in range(16):
        note[0, 1:6, 16 * i : 16 * i + 16] = bias[...]
    row = lax.broadcasted_iota(jnp.int32, (8, 256), 0)
    lane = lax.broadcasted_iota(jnp.int32, (8, 256), 1)
    mine = (lane >= s * 16) & (lane < s * 16 + 16)
    note[0] = jnp.where(row == 0, pool_part, jnp.where(mine, note[0], 0.0))
    note_first(0)

    respond(0, 0, 2)
    step1(3)
    note_second(0)
    respond(0, 2, 4)
    respond(1, 0, 2)
    step1(0)
    step2(3)
    respond(1, 2, 4)

    @pl.loop(1, 8)
    def _(o):
        links.arrived(proj_part(((chip + 8 - o) % 8) * 2 + core), wp_r.at[o])
        proj_forward(o).start()

    respond(2, 0, 2)
    step1(1)
    step2(0)
    respond(2, 2, 4)
    step3(3)
    turn(0, 2)
    step1(2)
    step2(1)
    turn(2, 4)
    step3(0)
    step2(2)

    @pl.loop(0, 8)
    def _(o):
        links.arrived(proj_part(((chip + 8 - o) % 8) * 2 + 1 - core), wf_r.at[o])

    head_note = note_total(0)
    pool_pre = head_note[0:1] + head_note[5:6]
    pool_act = jnp.broadcast_to(jax.nn.silu(pool_pre).astype(bf16).astype(f32), (ROWS, 256)).astype(bf16)

    def absorb(k):
        pre = step4(k) + head_note[1 + k : 2 + k]
        sigma = jax.nn.sigmoid(pre)
        slopes[k] = sigma * (1.0 + pre * (1.0 - sigma))
        act = (pre * sigma).astype(bf16)
        acts[k] = act
        return dot(act, wp[k])

    head = bias_proj[...] + dot(pool_act, wp[4])
    head = head + absorb(3)
    turn(4, 6)
    step3(1)
    head = head + absorb(0)
    head = head + absorb(1)
    step3(2)
    head = head + absorb(2)
    sigma = jax.nn.sigmoid(head)
    grad_f = cot[...].astype(f32) * (sigma * (1.0 + head * (1.0 - sigma)))
    grad = grad_f.astype(bf16)

    def block(k, n):
        if k < 3:
            return gp.at[k, pl.ds(aligned(PAD + n * ROWS), ROWS)]
        return g3.at[pl.ds(aligned(n * ROWS), ROWS)]

    def pass_on(k, n, slot, to):
        b = block(k, n)
        links.send(b, b, ag_s.at[k, slot], ag_r.at[k, n], space=to)

    def have(k, n):
        links.arrived(block(k, n), ag_r.at[k, n])

    def own_block(k):
        g = (dot_nt(grad, wp[k]) * slopes[k]).astype(bf16)
        if k < 3:
            gp[k, pl.ds(aligned(PAD + s * ROWS), ROWS)] = g
        else:
            g3[pl.ds(aligned(s * ROWS), ROWS)] = g
        pass_on(k, s, 0, other_z)
        pass_on(k, s, 1, right)
        pass_on(k, s, 2, left)
        pass_on(k, s, 3, sibling)
        note[1, k : k + 1] = jnp.sum(g.astype(f32), axis=0, keepdims=True)

    def gather1(k):
        n = at(1 - cz, cx, core)
        have(k, n)
        pass_on(k, n, 4, right)
        pass_on(k, n, 5, left)
        pass_on(k, n, 6, sibling)

    def gather2(k):
        n = at(0, xm, core)
        have(k, n)
        pass_on(k, n, 7, right)
        pass_on(k, n, 8, sibling)
        n = at(1, xp, core)
        have(k, n)
        pass_on(k, n, 9, left)
        pass_on(k, n, 10, sibling)
        n = at(1, xm, core)
        have(k, n)
        pass_on(k, n, 11, sibling)
        n = at(0, xp, core)
        have(k, n)
        pass_on(k, n, 12, sibling)

    def gather3(k):
        for z in range(2):
            n = at(z, x2, core)
            have(k, n)
            pass_on(k, n, 13 + z, sibling)
        for z in range(2):
            for col in (cx, xp, xm, x2):
                have(k, at(z, col, 1 - core))

    own_block(0)
    own_block(1)
    own_block(2)
    head_out[...] = (head * sigma).astype(bf16)
    for k in range(5):
        act = acts[k] if k < 4 else pool_act
        g = lax.dot_general(act, grad, TN, preferred_element_type=f32).astype(bf16).reshape(8, 2, 16, 256)
        gpo[0, k] = g[:, 0]
        gpo[1, k] = g[:, 1]
    links.send(gpo.at[1 - core], gpi, gp_s.at[0], gp_r.at[0], space=sibling)
    gather1(0)
    note[1, 4:5] = jnp.sum(dot_nt(grad, wp[4]), axis=0, keepdims=True)
    note[1, 5:6] = jnp.sum(grad.astype(f32), axis=0, keepdims=True)
    note[1, 6:8] = jnp.zeros((2, 256), f32)
    gather1(1)
    gather2(0)
    gather1(2)
    own_block(3)
    note_first(1)
    gather2(1)
    gather3(0)

    dws = (dw0, dw1, dw2, dw3)
    outs = (d0, d1, d2, d3)
    u1s, u1r = (u1s0, u1s1, u1s2, u1s3), (u1r0, u1r1, u1r2, u1r3)
    u2s, u2r = (u2s0, u2s1, u2s2, u2s3), (u2r0, u2r1, u2r2, u2r3)
    es, zr, zt = (es0, es1, es2, es3), (zr0, zr1, zr2, zr3), (zt0, zt1, zt2, zt3)

    def weight_grad(k):
        d = 48 * dilations[k]
        for a, (lo, hi) in enumerate(
            ((0, -((d - PIX) // 128) * 128), (0, PIX), (d // 128 * 128, PIX))
        ):
            g0 = PAD + lo - (a - 1) * d
            dws[k][384 * a : 384 * (a + 1)] = dot(xt[k, :, lo:hi], gp[k, g0 : g0 + hi - lo])

    def sum1(k):
        h = HALVES[k]
        dw = dws[k]
        u1s[k][0] = dw[pl.ds(aligned(y2 * 2 * h), h)].astype(bf16)
        links.send(u1s[k].at[0], u1r[k].at[0], ar_s.at[k, 0], ar_r.at[k, 0], dp=up)
        u1s[k][1] = dw[pl.ds(aligned(y2 * 2 * h + h), h)].astype(bf16)
        links.send(u1s[k].at[1], u1r[k].at[1], ar_s.at[k, 1], ar_r.at[k, 1], dp=down)

    def sum2(k):
        h = HALVES[k]
        dw = dws[k]
        links.arrived(u1r[k].at[0], ar_r.at[k, 0])
        u2s[k][0, 0] = (dw[pl.ds(aligned(yp * 2 * h), h)] + u1r[k][0].astype(f32)).astype(bf16)
        u2s[k][0, 1] = dw[pl.ds(aligned(yp * 2 * h + h), h)].astype(bf16)
        links.send(u2s[k].at[0], u2r[k].at[0], ar_s.at[k, 2], ar_r.at[k, 2], dp=up)
        links.arrived(u1r[k].at[1], ar_r.at[k, 1])
        u2s[k][1, 0] = dw[pl.ds(aligned(ym * 2 * h), h)].astype(bf16)
        u2s[k][1, 1] = (dw[pl.ds(aligned(ym * 2 * h + h), h)] + u1r[k][1].astype(f32)).astype(bf16)
        links.send(u2s[k].at[1], u2r[k].at[1], ar_s.at[k, 3], ar_r.at[k, 3], dp=down)

    def sum3(k):
        h = HALVES[k]
        dw = dws[k]
        links.arrived(u2r[k].at[0], ar_r.at[k, 2])
        links.arrived(u2r[k].at[1], ar_r.at[k, 3])
        for half in range(2):
            v = dw[pl.ds(aligned(y * 2 * h + half * h), h)] + (
                u2r[k][0, half].astype(f32) + u2r[k][1, half].astype(f32)
            )
            for lanes in range(2):
                quarter = v[:, 128 * lanes : 128 * (lanes + 1)]
                own[k, 2 * half + lanes, 0:h] = quarter
                es[k][2 * half + lanes] = quarter.astype(bf16)
        for o in range(1, 4):
            q = (hz + o) % 4
            links.send(es[k].at[q], zr[k].at[o - 1], ar_s.at[k, 3 + o], ar_r.at[k, 3 + o], dp=q * 4 + y)

    def sum4(k):
        h = HALVES[k]
        v = own[k, hz, 0:h]
        for o in range(1, 4):
            links.arrived(zr[k].at[o - 1], ar_r.at[k, 3 + o])
            v = v + zr[k][o - 1].astype(f32)
        zt[k][hz] = v.astype(bf16)
        for o in range(1, 4):
            q = (hz + o) % 4
            links.send(zt[k].at[hz], zt[k].at[hz], ar_s.at[k, 6 + o], ar_r.at[k, 6 + o], dp=q * 4 + y)

    def chunk(k, n):
        h = HALVES[k]
        return outs[k].at[pl.ds(aligned(n * 2 * h), 2 * h)]

    def half_chunk(k, n, half):
        h = HALVES[k]
        return outs[k].at[pl.ds(aligned(n * 2 * h + half * h), h)]

    def sum5(k):
        h = HALVES[k]
        for o in range(1, 4):
            links.arrived(zt[k].at[(hz + 4 - o) % 4], ar_r.at[k, 6 + o])
        for half in range(2):
            outs[k][pl.ds(aligned(y * 2 * h + half * h), h)] = jnp.concatenate(
                [zt[k][2 * half], zt[k][2 * half + 1]], axis=1
            )
        share = chunk(k, y)
        links.send(share, share, ar_s.at[k, 10], ar_r.at[k, 10], dp=up)
        links.send(share, share, ar_s.at[k, 11], ar_r.at[k, 11], dp=down)

    def sum6(k):
        links.arrived(chunk(k, ym), ar_r.at[k, 10])
        b = half_chunk(k, ym, 0)
        links.send(b, b, ar_s.at[k, 12], ar_r.at[k, 12], dp=up)
        links.arrived(chunk(k, yp), ar_r.at[k, 11])
        b = half_chunk(k, yp, 1)
        links.send(b, b, ar_s.at[k, 13], ar_r.at[k, 13], dp=down)

    def sum7(k):
        links.arrived(half_chunk(k, y2, 0), ar_r.at[k, 12])
        links.arrived(half_chunk(k, y2, 1), ar_r.at[k, 13])

    def proj_grad_copy(o):
        j = (chip + o) % 8
        return links.copy(gps.at[:, j], gpr.at[chip], gp_s.at[o], gp_r.at[o], dp, j * 2 + core)

    weight_grad(0)
    sum1(0)
    gather2(2)
    note_second(1)
    links.arrived(gpi, gp_r.at[0])
    gps[...] = (gpo[core].astype(f32) + gpi[...].astype(f32)).astype(bf16)

    @pl.loop(1, 8)
    def _(o):
        proj_grad_copy(o).start()

    gather1(3)
    gather3(1)
    weight_grad(1)
    sum1(1)
    sum2(0)
    gather2(3)
    gather3(2)
    weight_grad(2)
    sum1(2)
    sum2(1)
    sum3(0)
    gather3(3)

    dw3[0:128] = dot(xt[0, 128:256, :], g3[...])
    totals = note_total(1)
    pool_grad = (silu_slope(pool_pre) * totals[4:5]).astype(bf16)
    pool_row = pool_grad.astype(f32)
    column = jnp.transpose(jnp.broadcast_to(pooled[0:1].astype(f32), (128, 128)))
    dw3[128:256] = jnp.concatenate([column, column], axis=1) * pool_row

    @pl.loop(1, 8)
    def _(o):
        links.arrived(gpr.at[(chip + 8 - o) % 8], gp_r.at[o])

    gpr[pl.ds(chip, 1)] = gps[:, pl.ds(chip, 1)].reshape(1, 5, 16, 256)
    dw3[256:336] = lax.fori_loop(
        0, 8, lambda i, v: v + gpr[i].astype(f32).reshape(80, 256), jnp.zeros((80, 256), f32)
    )
    dw3[336:384] = jnp.zeros((48, 256), f32)
    dw3[336:340] = totals[0:4]
    dw3[340:341] = pool_row
    dw3[341:342] = totals[5:6]
    sum1(3)

    back = dot_nt(jnp.broadcast_to(pool_row, (16, 256)).astype(bf16), w_pool[...])[0:1] / PIX

    def input_grad(i):
        size = SMALL_BLOCK
        st = i * size
        result = dot_nt(g3[st : st + size], w_point[...]) + back
        for k in range(3):
            d = 48 * dilations[k]
            sides = 0.0
            for a in range(3):
                g0 = PAD + st - (a - 1) * d
                g = gp[k, g0 : g0 + size]
                tap = 384 * a
                ends = jnp.concatenate([w[k, tap : tap + 128], w[k, tap + 256 : tap + 384]], axis=0)
                sides = sides + dot_nt(g, ends)
                result = result + dot_nt(g, w[k, tap + 128 : tap + 256])
            result = result + shifted(sides[:, 0:128], dilations[k], size // 48, 1)
            result = result + shifted(sides[:, 128:256], dilations[k], size // 48, -1)
        gx[st : st + size] = result.astype(bf16)
        for j in range(size // ROWS):
            n = i * (size // ROWS) + j

            @pl.when(s != n)
            def _():
                gx_copy(n).start()

    def gx_copy(n):
        return links.copy(
            gx.at[pl.ds(n * ROWS, ROWS)], maps_out.at[:, pl.ds(aligned(s * 128, 128), 128)],
            gx_s.at[n], gx_r.at[s], dp, n,
        )

    input_grad(0)
    sum2(2)
    input_grad(1)
    sum3(1)
    sum2(3)
    input_grad(2)
    sum4(0)
    input_grad(3)
    sum3(2)
    sum3(3)
    input_grad(4)
    sum4(1)
    input_grad(5)
    sum5(0)
    sum4(2)
    sum4(3)
    input_grad(6)
    sum5(1)
    sum6(0)
    input_grad(7)
    sum5(2)
    sum5(3)
    sum6(1)
    sum7(0)
    maps_out[:, pl.ds(aligned(s * 128, 128), 128)] = gx[pl.ds(aligned(s * ROWS), ROWS)]
    sum6(2)
    sum6(3)

    @pl.loop(1, 16)
    def _(o):
        t = (s + o) % 16
        links.arrived(maps_out.at[:, pl.ds(aligned(t * 128, 128), 128)], gx_r.at[t])
        map_copy(o).wait_send()
        links.copy(
            gx.at[pl.ds(0, ROWS)], gx.at[pl.ds(0, ROWS)], gx_s.at[t], gx_s.at[t], dp, t
        ).wait_send()

    proj_forward(0).wait_send()

    @pl.loop(1, 8)
    def _(o):
        proj_copy(o).wait_send()
        proj_forward(o).wait_send()
        note_copy(0, o).wait_send()
        note_copy(1, o).wait_send()
        proj_grad_copy(o).wait_send()

    sum7(1)
    sum7(2)
    sum7(3)
    links.flush()


def finish_kernel(head, d0, d1, d2, d3, maps, head_out, maps_out, atrous, point, pool, bias, proj, proj_bias):
    s = lax.axis_index("space")
    head_out[...] = head[...]
    maps_out[...] = maps[...]
    for k, d in enumerate((d0, d1, d2)):
        atrous[k] = d[...].astype(f32)
    point[...] = d3[0:128].astype(f32)
    pool[...] = d3[128:256].astype(f32)
    proj[...] = d3[256:336].astype(f32)
    rows = d3[336:352].astype(f32)
    picked = jnp.zeros((5, 16), f32)
    for i in range(16):
        picked = jnp.where(s == i, rows[0:5, 16 * i : 16 * i + 16], picked)
    bias[...] = picked
    proj_bias[...] = rows[5:6]


def dma(*shape):
    return pltpu.SemaphoreType.DMA(shape)


def vm(dtype, *shape):
    return pltpu.VMEM(shape, dtype)


def body(feature_maps, w_atrous, w_point, w_pool, bias_branch, w_proj, bias_proj, cotangent):
    vmem = pl.BlockSpec(memory_space=pltpu.VMEM)
    shape = jax.ShapeDtypeStruct
    sizes = [8 * h for h in HALVES]
    results = pl.pallas_call(
        aspp_kernel,
        out_shape=(
            shape((ROWS, 256), bf16), *[shape((n, 256), bf16) for n in sizes], shape((ROWS, 2048), bf16),
        ),
        in_specs=[vmem] * 8,
        out_specs=[vmem] * 6,
        scratch_shapes=[
            vm(bf16, PIX, 128), vm(bf16, 3, PIX + 2 * PAD, 384),
            vm(bf16, 4, 8, ROWS, 256), vm(bf16, 4, 8, ROWS, 256), vm(f32, 4, 8, ROWS, 256),
            vm(bf16, 4, ROWS, 256), vm(bf16, 4, ROWS, 256), vm(bf16, 4, ROWS, 256), vm(bf16, 4, ROWS, 256),
            vm(bf16, 4, 2, ROWS, 256), vm(bf16, 4, 2, ROWS, 256),
            vm(bf16, 4, 2, ROWS, 256), vm(bf16, 4, 2, ROWS, 256),
            vm(bf16, 4, ROWS, 256), vm(bf16, 4, ROWS, 256), vm(bf16, 5, 256, 256),
            vm(f32, 4, ROWS, 256), vm(bf16, 4, ROWS, 256),
            vm(bf16, 3, PIX + 2 * PAD, 256), vm(bf16, PIX, 256), vm(bf16, 3, 384, PIX),
            *[vm(f32, n, 256) for n in sizes],
            *[vm(bf16, 2, h, 256) for h in HALVES], *[vm(bf16, 2, h, 256) for h in HALVES],
            *[vm(bf16, 2, 2, h, 256) for h in HALVES], *[vm(bf16, 2, 2, h, 256) for h in HALVES],
            *[vm(bf16, 4, h, 128) for h in HALVES], *[vm(bf16, 3, h, 128) for h in HALVES],
            *[vm(bf16, 4, h, 128) for h in HALVES],
            vm(f32, 4, 4, 144, 128),
            vm(bf16, 2, 5, 8, 16, 256), vm(bf16, 5, 8, 16, 256), vm(bf16, 5, 8, 16, 256),
            vm(bf16, 8, 5, 16, 256),
            vm(f32, 2, 8, 256), vm(f32, 2, 8, 256), vm(f32, 2, 8, 256), vm(f32, 2, 8, 8, 256),
            vm(bf16, PIX, 128),
            dma(16), dma(16), dma(8), dma(8), dma(8), dma(8), dma(4, 6), dma(4, 6),
            dma(4, 15), dma(4, 16), dma(4, 14), dma(4, 14),
            dma(8), dma(8), dma(2, 9), dma(2, 9), dma(16), dma(16),
        ],
        compiler_params=pltpu.CompilerParams(
            collective_id=0, has_side_effects=True, vmem_limit_bytes=VMEM_LIMIT
        ),
        name="aspp",
    )(
        feature_maps.reshape(ROWS, 2048), w_atrous.reshape(3, 1152, 256), w_point, w_pool, bias_branch,
        w_proj, bias_proj.reshape(1, 256), cotangent.reshape(ROWS, 256),
    )
    head_out, grad_maps, atrous, point, pool, bias, proj, proj_bias = pl.pallas_call(
        finish_kernel,
        out_shape=(
            shape((ROWS, 256), bf16), shape((ROWS, 2048), bf16), shape((3, 1152, 256), f32),
            shape((128, 256), f32), shape((128, 256), f32), shape((5, 16), f32), shape((80, 256), f32),
            shape((1, 256), f32),
        ),
        in_specs=[vmem] * 6,
        out_specs=[vmem] * 8,
        compiler_params=pltpu.CompilerParams(vmem_limit_bytes=VMEM_LIMIT),
        name="finish",
    )(*results)
    return (
        head_out.reshape(1, 3, 48, 256),
        grad_maps.reshape(1, 3, 48, 2048),
        atrous.reshape(3, 9, 128, 256),
        point,
        pool,
        bias,
        proj.reshape(5, 16, 256),
        proj_bias.reshape(256),
    )


def solution(mesh):
    placed = (
        P("dp", "space", None, None),
        P(None, None, "space", None),
        P("space", None),
        P("space", None),
        P(None, "space"),
        P(None, "space", None),
        P(),
        P("dp", "space", None, None),
    )
    return jax.shard_map(
        body,
        mesh=mesh,
        in_specs=placed,
        out_specs=(
            P("dp", "space", None, None),
            P("dp", "space", None, None),
            P(None, None, "space", None),
            P("space", None),
            P("space", None),
            P(None, "space"),
            P(None, "space", None),
            P(),
        ),
        check_vma=False,
    )
```

```python
import jax
import jax.numpy as jnp
from jax import lax
from jax.experimental import pallas as pl
from jax.experimental.pallas import tpu as pltpu
from jax.sharding import PartitionSpec as P

bf16 = jnp.bfloat16
f32 = jnp.float32
dilations = (6, 12, 18)
MESH = pl.DeviceIdType.MESH
ROWS = 144
PIX = 2304
PAD = 864
NT = (((1,), (1,)), ((), ()))
TN = (((0,), (0,)), ((), ()))
BLOCK = 576
VMEM_LIMIT = 60 * 2**20


def silu_slope(values):
    sigma = jax.nn.sigmoid(values)
    return sigma * (1.0 + values * (1.0 - sigma))


def dot(a, b):
    return jnp.dot(a, b, preferred_element_type=f32)


def dot_nt(a, b):
    return lax.dot_general(a, b, NT, preferred_element_type=f32)


def aligned(value, step=16):
    return value if isinstance(value, int) else pl.multiple_of(value, step)


class Links:
    def __init__(self, dp, space):
        self.dp = dp
        self.space = space
        self.sent = []

    def copy(self, src, dst, ssem, rsem, dp, space):
        return pltpu.make_async_remote_copy(
            src_ref=src, dst_ref=dst, send_sem=ssem, recv_sem=rsem, device_id=(dp, space), device_id_type=MESH
        )

    def send(self, src, dst, ssem, rsem, dp=None, space=None):
        c = self.copy(src, dst, ssem, rsem, self.dp if dp is None else dp, self.space if space is None else space)
        c.start()
        self.sent.append(c)

    def arrived(self, ref, rsem):
        self.copy(ref, ref, rsem, rsem, self.dp, self.space).wait_recv()

    def flush(self):
        for c in self.sent:
            c.wait_send()


def shifted(block, d, rows, sign):
    lanes = block.shape[1]
    v = block.reshape(rows, 48, lanes)
    col = lax.broadcasted_iota(jnp.int32, (rows, 48, lanes), 1)
    if sign < 0:
        v = jnp.where(col >= d, pltpu.roll(v, d, 1), 0.0)
    else:
        v = jnp.where(col < 48 - d, pltpu.roll(v, 48 - d, 1), 0.0)
    return v.reshape(rows * 48, lanes)


PIECES = ((0, 0, 2, 96), (0, 2, 3, 48), (1, 0, 2, 96), (1, 2, 3, 48), (2, 0, 2, 96), (2, 2, 3, 48), (3, 0, 1, 48))
HALVES = tuple(piece[3] for piece in PIECES)
CUT = 80
SMALL_BLOCK = 288


def aspp_kernel(
    maps_in, w_in, w_point_in, w_pool_in, bias_in, w_proj_in, bias_proj_in, cot_in,
    head_to, d_to, d3_to, maps_out,
    maps, w, w_point, w_pool, bias, w_proj, bias_proj, cot, head_out, d, d3,
    x, c, core_out, core_in, acc, sa, sb, ra, rb, s2p, s2m, r2p, r2m, sz, rz, zs, zin, wp, slopes, acts,
    gp, g3, xt, dw, dw3, own, gpo, gpi, gps, gpr, note, note_in, note_sum, notes, gx,
    in_s, out_s, x_s, x_r, wp_s, wp_r, wf_s, wf_r, rs_s, rs_r,
    ag_s, ag_r, ar_s, ar_r, gp_s, gp_r, note_s, note_r, gx_s, gx_r, *pieces,
):
    u1s, u1r, u2s, u2r, es, zr, zt = [pieces[7 * i : 7 * i + 7] for i in range(7)]
    dp = lax.axis_index("dp")
    s = lax.axis_index("space")
    core = s % 2
    chip = s // 2
    cx = chip % 4
    cz = chip // 4
    xp = (cx + 1) % 4
    xm = (cx + 3) % 4
    x2 = (cx + 2) % 4

    def at(z, col, half):
        return (z * 4 + col) * 2 + half

    right = at(cz, xp, core)
    left = at(cz, xm, core)
    other_z = at(1 - cz, cx, core)
    sibling = at(cz, cx, 1 - core)
    y = dp % 4
    hz = dp // 4
    yp = (y + 1) % 4
    ym = (y + 3) % 4
    y2 = (y + 2) % 4
    up = hz * 4 + yp
    down = hz * 4 + ym
    links = Links(dp, s)

    loads = [
        pltpu.make_async_copy(source, target, in_s.at[i])
        for i, (source, target) in enumerate((
            (maps_in, maps), (w_proj_in, w_proj), (w_point_in, w_point), (w_pool_in, w_pool), (bias_in, bias),
            (bias_proj_in, bias_proj), (cot_in, cot), (w_in, w),
        ))
    ]
    for load in loads:
        load.start()
    barrier = pltpu.get_barrier_semaphore()

    @pl.loop(1, 16)
    def _(o):
        pl.semaphore_signal(barrier, inc=1, device_id=(dp, (s + o) % 16), device_id_type=MESH)

    pl.semaphore_signal(barrier, inc=1, device_id=(up, s), device_id_type=MESH)
    pl.semaphore_signal(barrier, inc=1, device_id=(down, s), device_id_type=MESH)
    for o in range(1, 4):
        pl.semaphore_signal(barrier, inc=1, device_id=(((hz + o) % 4) * 4 + y, s), device_id_type=MESH)
    pl.semaphore_wait(barrier, 20)

    def map_copy(o):
        t = (s + o) % 16
        return links.copy(
            maps.at[:, pl.ds(aligned(t * 128, 128), 128)], x.at[pl.ds(aligned(s * ROWS), ROWS)],
            x_s.at[o], x_r.at[o], dp, t,
        )

    loads[0].wait()

    @pl.loop(1, 16)
    def _(o):
        map_copy(o).start()

    for load in loads[1:7]:
        load.wait()

    x[pl.ds(aligned(s * ROWS), ROWS)] = maps[:, pl.ds(aligned(s * 128, 128), 128)]
    wp[:, pl.ds(aligned(s * 16), 16)] = w_proj[...]
    for k in range(3):
        c[k, 0:PAD] = jnp.zeros((PAD, 384), bf16)
        c[k, PAD + PIX : PAD + PIX + PAD] = jnp.zeros((PAD, 384), bf16)
        gp[k, 0:PAD] = jnp.zeros((PAD, 256), bf16)
        gp[k, PAD + PIX : PAD + PIX + PAD] = jnp.zeros((PAD, 256), bf16)

    def build(o, total):
        t = (s + 16 - o) % 16
        base = aligned(t * ROWS)
        raw = x[pl.ds(base, ROWS)]
        v = raw.astype(f32)
        for k, d in enumerate(dilations):
            lo = shifted(v, d, 3, -1).astype(bf16)
            hi = shifted(v, d, 3, 1).astype(bf16)
            c[k, pl.ds(aligned(PAD + base), ROWS)] = jnp.concatenate([lo, raw, hi], axis=1)
        return total + jnp.sum(v.reshape(18, 8, 128), axis=0)

    total = build(0, jnp.zeros((8, 128), f32))

    def build_remote(o, total):
        t = (s + 16 - o) % 16
        links.arrived(x.at[pl.ds(aligned(t * ROWS), ROWS)], x_r.at[o])
        return build(o, total)

    total = lax.fori_loop(1, 16, build_remote, total)

    def proj_part(t):
        return wp.at[:, pl.ds(aligned(t * 16), 16)]

    def proj_copy(o):
        t = ((chip + o) % 8) * 2 + core
        return links.copy(proj_part(s), proj_part(s), wp_s.at[o], wp_r.at[o], dp, t)

    def proj_forward(o):
        t = ((chip + 8 - o) % 8) * 2 + core
        return links.copy(proj_part(t), proj_part(t), wf_s.at[o], wf_r.at[o], dp, sibling)

    @pl.loop(1, 8)
    def _(o):
        proj_copy(o).start()

    proj_forward(0).start()

    def note_first(n):
        links.send(note.at[n], note_in.at[n], note_s.at[n, 8], note_r.at[n, 8], space=sibling)

    def note_copy(n, o):
        t = ((chip + o) % 8) * 2 + core
        return links.copy(note_sum.at[n], notes.at[n, chip], note_s.at[n, o], note_r.at[n, o], dp, t)

    def note_second(n):
        links.arrived(note_in.at[n], note_r.at[n, 8])
        note_sum[n] = note[n] + note_in[n]
        notes[n, pl.ds(chip, 1)] = note_sum[n][None]

        @pl.loop(1, 8)
        def _(o):
            note_copy(n, o).start()

    def note_total(n):
        @pl.loop(1, 8)
        def _(o):
            links.arrived(notes.at[n, (chip + 8 - o) % 8], note_r.at[n, o])

        return lax.fori_loop(0, 8, lambda i, v: v + notes[n, i], jnp.zeros((8, 256), f32))

    def respond(k, lo, hi):
        @pl.loop(lo, hi)
        def _(i):
            base = aligned(i * BLOCK)
            if k < 3:
                d = dilations[k] * 48
                lhs = jnp.concatenate(
                    [c[k, pl.ds(aligned(PAD + base + (a - 1) * d), BLOCK)] for a in range(3)], axis=1
                )
                p = dot(lhs, w[k])
            else:
                p = dot(c[0, pl.ds(aligned(PAD + base), BLOCK), 128:256], w_point[...])
            p = p.reshape(2, 2, ROWS, 256)
            first = core == 0
            acc[k, pl.ds(i * 2, 2)] = jnp.where(first, p[:, 0], p[:, 1])
            core_out[k, pl.ds(i * 2, 2)] = jnp.where(first, p[:, 1], p[:, 0]).astype(bf16)

        if hi == PIX // BLOCK:
            links.send(core_out.at[k], core_in.at[k], rs_s.at[k, 0], rs_r.at[k, 0], space=sibling)

    def step1(k):
        links.arrived(core_in.at[k], rs_r.at[k, 0])

        @pl.loop(0, 8)
        def _(j):
            acc[k, j] = acc[k, j] + core_in[k, j].astype(f32)

        sa[k] = acc[k, x2].astype(bf16)
        links.send(sa.at[k], ra.at[k], rs_s.at[k, 1], rs_r.at[k, 1], space=right)
        sb[k] = acc[k, 4 + x2].astype(bf16)
        links.send(sb.at[k], rb.at[k], rs_s.at[k, 2], rs_r.at[k, 2], space=left)

    def cross1(k):
        links.arrived(core_in.at[k], rs_r.at[k, 0])

        @pl.loop(0, 8)
        def _(j):
            acc[k, j] = acc[k, j] + core_in[k, j].astype(f32)

        @pl.loop(0, 4)
        def _(j):
            zs[j] = acc[k, (1 - cz) * 4 + j].astype(bf16)

        links.send(zs, zin, rs_s.at[k, 1], rs_r.at[k, 1], space=other_z)

    def cross2(k):
        links.arrived(zin, rs_r.at[k, 1])

        @pl.loop(0, 4)
        def _(j):
            acc[k, cz * 4 + j] = acc[k, cz * 4 + j] + zin[j].astype(f32)

        sa[k] = acc[k, cz * 4 + x2].astype(bf16)
        upper, lower = pl.ds(0, CUT), pl.ds(CUT, ROWS - CUT)
        links.send(sa.at[k, upper], ra.at[k, upper], rs_s.at[k, 2], rs_r.at[k, 2], space=right)
        links.send(sa.at[k, lower], ra.at[k, lower], rs_s.at[k, 3], rs_r.at[k, 3], space=left)

    def cross3(k):
        links.arrived(ra.at[k, pl.ds(0, CUT)], rs_r.at[k, 2])
        s2p[k, 0, 0:CUT] = (acc[k, cz * 4 + xp, 0:CUT] + ra[k, 0:CUT].astype(f32)).astype(bf16)
        s2p[k, 0, CUT:ROWS] = acc[k, cz * 4 + xp, CUT:ROWS].astype(bf16)
        links.send(s2p.at[k, 0], r2p.at[k, 0], rs_s.at[k, 4], rs_r.at[k, 4], space=right)
        links.arrived(ra.at[k, pl.ds(CUT, ROWS - CUT)], rs_r.at[k, 3])
        s2m[k, 0, 0:CUT] = acc[k, cz * 4 + xm, 0:CUT].astype(bf16)
        s2m[k, 0, CUT:ROWS] = (acc[k, cz * 4 + xm, CUT:ROWS] + ra[k, CUT:ROWS].astype(f32)).astype(bf16)
        links.send(s2m.at[k, 0], r2m.at[k, 0], rs_s.at[k, 5], rs_r.at[k, 5], space=left)

    def cross4(k):
        links.arrived(r2p.at[k, 0], rs_r.at[k, 4])
        links.arrived(r2m.at[k, 0], rs_r.at[k, 5])
        return acc[k, cz * 4 + cx] + (r2p[k, 0].astype(f32) + r2m[k, 0].astype(f32))

    def step2(k):
        links.arrived(ra.at[k], rs_r.at[k, 1])
        s2p[k, 0] = (acc[k, xp] + ra[k].astype(f32)).astype(bf16)
        s2p[k, 1] = acc[k, 4 + xp].astype(bf16)
        links.send(s2p.at[k], r2p.at[k], rs_s.at[k, 3], rs_r.at[k, 3], space=right)
        links.arrived(rb.at[k], rs_r.at[k, 2])
        s2m[k, 0] = acc[k, xm].astype(bf16)
        s2m[k, 1] = (acc[k, 4 + xm] + rb[k].astype(f32)).astype(bf16)
        links.send(s2m.at[k], r2m.at[k], rs_s.at[k, 4], rs_r.at[k, 4], space=left)

    def step3(k):
        links.arrived(r2p.at[k], rs_r.at[k, 3])
        links.arrived(r2m.at[k], rs_r.at[k, 4])
        for z in range(2):
            acc[k, z * 4 + cx] = acc[k, z * 4 + cx] + (r2p[k, z].astype(f32) + r2m[k, z].astype(f32))
        sz[k] = acc[k, (1 - cz) * 4 + cx].astype(bf16)
        links.send(sz.at[k], rz.at[k], rs_s.at[k, 5], rs_r.at[k, 5], space=other_z)

    def step4(k):
        links.arrived(rz.at[k], rs_r.at[k, 5])
        return acc[k, cz * 4 + cx] + rz[k].astype(f32)

    def turn(lo, hi):
        @pl.loop(lo, hi)
        def _(i):
            st = aligned(i * 384, 128)
            v = x[pl.ds(st, 384)].astype(f32)
            mid = jnp.transpose(v).astype(bf16)
            for k, d in enumerate(dilations):
                xt[k, 0:128, pl.ds(st, 384)] = jnp.transpose(shifted(v, d, 8, -1)).astype(bf16)
                xt[k, 128:256, pl.ds(st, 384)] = mid
                xt[k, 256:384, pl.ds(st, 384)] = jnp.transpose(shifted(v, d, 8, 1)).astype(bf16)

    respond(3, 0, 4)

    pooled = (jnp.sum(total, axis=0, keepdims=True) / PIX).astype(bf16)
    pooled = jnp.broadcast_to(pooled, (16, 128))
    pool_part = dot(pooled, w_pool[...])[0:8]
    note[0] = jnp.zeros((8, 256), f32)
    for i in range(16):
        note[0, 1:6, 16 * i : 16 * i + 16] = bias[...]
    row = lax.broadcasted_iota(jnp.int32, (8, 256), 0)
    lane = lax.broadcasted_iota(jnp.int32, (8, 256), 1)
    mine = (lane >= s * 16) & (lane < s * 16 + 16)
    note[0] = jnp.where(row == 0, pool_part, jnp.where(mine, note[0], 0.0))
    note_first(0)

    loads[7].wait()
    respond(0, 0, 2)
    step1(3)
    note_second(0)
    respond(0, 2, 4)
    respond(1, 0, 2)
    step1(0)
    step2(3)
    respond(1, 2, 4)

    @pl.loop(1, 8)
    def _(o):
        links.arrived(proj_part(((chip + 8 - o) % 8) * 2 + core), wp_r.at[o])
        proj_forward(o).start()

    respond(2, 0, 2)
    cross1(1)
    step2(0)
    step3(3)
    respond(2, 2, 4)
    turn(0, 2)
    step1(2)
    turn(2, 4)
    cross2(1)
    step3(0)
    step2(2)

    @pl.loop(0, 8)
    def _(o):
        links.arrived(proj_part(((chip + 8 - o) % 8) * 2 + 1 - core), wf_r.at[o])

    head_note = note_total(0)
    pool_pre = head_note[0:1] + head_note[5:6]
    pool_act = jnp.broadcast_to(jax.nn.silu(pool_pre).astype(bf16).astype(f32), (ROWS, 256)).astype(bf16)

    def absorb(k):
        pre = (cross4(k) if k == 1 else step4(k)) + head_note[1 + k : 2 + k]
        sigma = jax.nn.sigmoid(pre)
        slopes[k] = sigma * (1.0 + pre * (1.0 - sigma))
        act = (pre * sigma).astype(bf16)
        acts[k] = act
        return dot(act, wp[k])

    head = bias_proj[...] + dot(pool_act, wp[4])
    head = head + absorb(3)
    turn(4, 6)
    cross3(1)
    step3(2)
    head = head + absorb(0)
    head = head + absorb(1)
    head = head + absorb(2)
    sigma = jax.nn.sigmoid(head)
    grad_f = cot[...].astype(f32) * (sigma * (1.0 + head * (1.0 - sigma)))
    grad = grad_f.astype(bf16)

    def block(k, n):
        if k < 3:
            return gp.at[k, pl.ds(aligned(PAD + n * ROWS), ROWS)]
        return g3.at[pl.ds(aligned(n * ROWS), ROWS)]

    def pass_on(k, n, slot, to):
        b = block(k, n)
        links.send(b, b, ag_s.at[k, slot], ag_r.at[k, n], space=to)

    def have(k, n):
        links.arrived(block(k, n), ag_r.at[k, n])

    def own_block(k):
        g = (dot_nt(grad, wp[k]) * slopes[k]).astype(bf16)
        if k < 3:
            gp[k, pl.ds(aligned(PAD + s * ROWS), ROWS)] = g
        else:
            g3[pl.ds(aligned(s * ROWS), ROWS)] = g
        pass_on(k, s, 0, other_z)
        pass_on(k, s, 1, right)
        pass_on(k, s, 2, left)
        pass_on(k, s, 3, sibling)
        note[1, k : k + 1] = jnp.sum(g.astype(f32), axis=0, keepdims=True)

    def head_store():
        head_out[...] = (head * sigma).astype(bf16)
        own_head().start()

    def gather1(k):
        n = at(1 - cz, cx, core)
        have(k, n)
        pass_on(k, n, 4, right)
        pass_on(k, n, 5, left)
        pass_on(k, n, 6, sibling)

    def gather2(k):
        n = at(0, xm, core)
        have(k, n)
        pass_on(k, n, 7, right)
        pass_on(k, n, 8, sibling)
        n = at(1, xp, core)
        have(k, n)
        pass_on(k, n, 9, left)
        pass_on(k, n, 10, sibling)
        n = at(1, xm, core)
        have(k, n)
        pass_on(k, n, 11, sibling)
        n = at(0, xp, core)
        have(k, n)
        pass_on(k, n, 12, sibling)

    def gather3(k):
        for z in range(2):
            n = at(z, x2, core)
            have(k, n)
            pass_on(k, n, 13 + z, sibling)

    def gather4(k):
        for z in range(2):
            for col in (cx, xp, xm, x2):
                have(k, at(z, col, 1 - core))

    def proj_grad():
        for k in range(5):
            act = acts[k] if k < 4 else pool_act
            g = lax.dot_general(act, grad, TN, preferred_element_type=f32).astype(bf16)
            g = g.reshape(8, 2, 16, 256)
            gpo[0, k] = g[:, 0]
            gpo[1, k] = g[:, 1]
        links.send(gpo.at[1 - core], gpi, gp_s.at[0], gp_r.at[0], space=sibling)

    def note_start():
        note[1, 4:5] = jnp.sum(dot_nt(grad, wp[4]), axis=0, keepdims=True)
        note[1, 5:6] = jnp.sum(grad.astype(f32), axis=0, keepdims=True)
        note[1, 6:8] = jnp.zeros((2, 256), f32)
        note_first(1)

    def weight_grad(p):
        k, first, last, _ = PIECES[p]
        d = 48 * dilations[k]
        for a, (lo, hi) in enumerate(
            ((0, -((d - PIX) // 128) * 128), (0, PIX), (d // 128 * 128, PIX))
        ):
            if first <= a < last:
                g0 = PAD + lo - (a - 1) * d
                dw[k, 384 * a : 384 * (a + 1)] = dot(xt[k, :, lo:hi], gp[k, g0 : g0 + hi - lo])

    def summed(p, start, size):
        k, first, _, _ = PIECES[p]
        if k == 3:
            return dw3[pl.ds(aligned(start), size)]
        return dw[k, pl.ds(aligned(384 * first + start), size)]

    def result(p, start, size):
        k, first, _, _ = PIECES[p]
        if k == 3:
            return d3.at[pl.ds(aligned(start), size)]
        return d.at[k, pl.ds(aligned(384 * first + start), size)]

    def sum1(k):
        h = HALVES[k]
        u1s[k][0] = summed(k, y2 * 2 * h, h).astype(bf16)
        links.send(u1s[k].at[0], u1r[k].at[0], ar_s.at[k, 0], ar_r.at[k, 0], dp=up)
        u1s[k][1] = summed(k, y2 * 2 * h + h, h).astype(bf16)
        links.send(u1s[k].at[1], u1r[k].at[1], ar_s.at[k, 1], ar_r.at[k, 1], dp=down)

    def sum2(k):
        h = HALVES[k]
        links.arrived(u1r[k].at[0], ar_r.at[k, 0])
        u2s[k][0, 0] = (summed(k, yp * 2 * h, h) + u1r[k][0].astype(f32)).astype(bf16)
        u2s[k][0, 1] = summed(k, yp * 2 * h + h, h).astype(bf16)
        links.send(u2s[k].at[0], u2r[k].at[0], ar_s.at[k, 2], ar_r.at[k, 2], dp=up)
        links.arrived(u1r[k].at[1], ar_r.at[k, 1])
        u2s[k][1, 0] = summed(k, ym * 2 * h, h).astype(bf16)
        u2s[k][1, 1] = (summed(k, ym * 2 * h + h, h) + u1r[k][1].astype(f32)).astype(bf16)
        links.send(u2s[k].at[1], u2r[k].at[1], ar_s.at[k, 3], ar_r.at[k, 3], dp=down)

    def sum3(k):
        h = HALVES[k]
        links.arrived(u2r[k].at[0], ar_r.at[k, 2])
        links.arrived(u2r[k].at[1], ar_r.at[k, 3])
        for half in range(2):
            v = summed(k, y * 2 * h + half * h, h) + (
                u2r[k][0, half].astype(f32) + u2r[k][1, half].astype(f32)
            )
            for lanes in range(2):
                quarter = v[:, 128 * lanes : 128 * (lanes + 1)]
                own[k, 2 * half + lanes, 0:h] = quarter
                es[k][2 * half + lanes] = quarter.astype(bf16)
        for o in range(1, 4):
            q = (hz + o) % 4
            links.send(es[k].at[q], zr[k].at[o - 1], ar_s.at[k, 3 + o], ar_r.at[k, 3 + o], dp=q * 4 + y)

    def sum4(k):
        h = HALVES[k]
        v = own[k, hz, 0:h]
        for o in range(1, 4):
            links.arrived(zr[k].at[o - 1], ar_r.at[k, 3 + o])
            v = v + zr[k][o - 1].astype(f32)
        zt[k][hz] = v.astype(bf16)
        for o in range(1, 4):
            q = (hz + o) % 4
            links.send(zt[k].at[hz], zt[k].at[hz], ar_s.at[k, 6 + o], ar_r.at[k, 6 + o], dp=q * 4 + y)

    def chunk(k, n):
        h = HALVES[k]
        return result(k, n * 2 * h, 2 * h)

    def half_chunk(k, n, half):
        h = HALVES[k]
        return result(k, n * 2 * h + half * h, h)

    def sum5(k):
        h = HALVES[k]
        for o in range(1, 4):
            links.arrived(zt[k].at[(hz + 4 - o) % 4], ar_r.at[k, 6 + o])
        for half in range(2):
            result(k, y * 2 * h + half * h, h)[...] = jnp.concatenate(
                [zt[k][2 * half], zt[k][2 * half + 1]], axis=1
            )
        share = chunk(k, y)
        links.send(share, share, ar_s.at[k, 10], ar_r.at[k, 10], dp=up)
        links.send(share, share, ar_s.at[k, 11], ar_r.at[k, 11], dp=down)

    def sum6(k):
        links.arrived(chunk(k, ym), ar_r.at[k, 10])
        b = half_chunk(k, ym, 0)
        links.send(b, b, ar_s.at[k, 12], ar_r.at[k, 12], dp=up)
        links.arrived(chunk(k, yp), ar_r.at[k, 11])
        b = half_chunk(k, yp, 1)
        links.send(b, b, ar_s.at[k, 13], ar_r.at[k, 13], dp=down)

    def store(p):
        k, first, last, _ = PIECES[p]
        if k == 3:
            return pltpu.make_async_copy(d3, d3_to, out_s.at[p])
        rows = pl.ds(384 * first, 384 * (last - first))
        return pltpu.make_async_copy(d.at[k, rows], d_to.at[k, rows], out_s.at[p])

    def sum7(k):
        links.arrived(half_chunk(k, y2, 0), ar_r.at[k, 12])
        links.arrived(half_chunk(k, y2, 1), ar_r.at[k, 13])
        store(k).start()

    def proj_grad_copy(o):
        j = (chip + o) % 8
        return links.copy(gps.at[:, j], gpr.at[chip], gp_s.at[o], gp_r.at[o], dp, j * 2 + core)

    def proj_grad_share():
        links.arrived(gpi, gp_r.at[0])
        gps[...] = (gpo[core].astype(f32) + gpi[...].astype(f32)).astype(bf16)

        @pl.loop(1, 8)
        def _(o):
            proj_grad_copy(o).start()

    def small_grads():
        dw3[0:128] = dot(xt[0, 128:256, :], g3[...])
        totals = note_total(1)
        pool_grad = (silu_slope(pool_pre) * totals[4:5]).astype(bf16)
        pool_row = pool_grad.astype(f32)
        column = jnp.transpose(jnp.broadcast_to(pooled[0:1].astype(f32), (128, 128)))
        dw3[128:256] = jnp.concatenate([column, column], axis=1) * pool_row

        @pl.loop(1, 8)
        def _(o):
            links.arrived(gpr.at[(chip + 8 - o) % 8], gp_r.at[o])

        gpr[pl.ds(chip, 1)] = gps[:, pl.ds(chip, 1)].reshape(1, 5, 16, 256)
        dw3[256:336] = lax.fori_loop(
            0, 8, lambda i, v: v + gpr[i].astype(f32).reshape(80, 256), jnp.zeros((80, 256), f32)
        )
        dw3[336:384] = jnp.zeros((48, 256), f32)
        dw3[336:340] = totals[0:4]
        dw3[340:341] = pool_row
        dw3[341:342] = totals[5:6]
        return dot_nt(jnp.broadcast_to(pool_row, (16, 256)).astype(bf16), w_pool[...])[0:1] / PIX

    def input_grad(i):
        size = SMALL_BLOCK
        st = i * size
        total = dot_nt(g3[st : st + size], w_point[...]) + back
        for k in range(3):
            d = 48 * dilations[k]
            sides = 0.0
            for a in range(3):
                g0 = PAD + st - (a - 1) * d
                g = gp[k, g0 : g0 + size]
                tap = 384 * a
                ends = jnp.concatenate([w[k, tap : tap + 128], w[k, tap + 256 : tap + 384]], axis=0)
                sides = sides + dot_nt(g, ends)
                total = total + dot_nt(g, w[k, tap + 128 : tap + 256])
            total = total + shifted(sides[:, 0:128], dilations[k], size // 48, 1)
            total = total + shifted(sides[:, 128:256], dilations[k], size // 48, -1)
        gx[st : st + size] = total.astype(bf16)
        for j in range(size // ROWS):
            n = i * (size // ROWS) + j

            @pl.when(s != n)
            def _():
                gx_copy(n).start()

    def gx_copy(n):
        return links.copy(
            gx.at[pl.ds(n * ROWS, ROWS)], maps_out.at[:, pl.ds(aligned(s * 128, 128), 128)],
            gx_s.at[n], gx_r.at[s], dp, n,
        )

    def own_maps():
        return pltpu.make_async_copy(
            gx.at[pl.ds(aligned(s * ROWS), ROWS)], maps_out.at[:, pl.ds(aligned(s * 128, 128), 128)], out_s.at[7]
        )

    def own_head():
        return pltpu.make_async_copy(head_out, head_to, out_s.at[8])

    def collect():
        own_maps().start()

        @pl.loop(1, 16)
        def _(o):
            t = (s + o) % 16
            links.arrived(maps_out.at[:, pl.ds(aligned(t * 128, 128), 128)], gx_r.at[t])

    own_block(0)
    own_block(1)
    gather1(0)
    gather1(1)
    own_block(2)
    gather2(0)
    proj_grad()
    head_store()
    gather2(1)
    gather1(2)
    own_block(3)
    gather3(0)
    note_start()
    gather4(0)
    weight_grad(0)
    gather3(1)
    gather1(3)
    sum1(0)
    gather2(2)
    gather4(1)
    weight_grad(2)
    sum1(2)
    weight_grad(3)
    sum2(0)
    gather2(3)
    proj_grad_share()
    weight_grad(1)
    gather3(2)
    sum1(1)
    sum2(2)
    sum1(3)
    gather4(2)
    note_second(1)
    weight_grad(4)
    sum3(0)
    sum2(1)
    gather3(3)
    sum1(4)
    weight_grad(5)
    sum3(2)
    gather4(3)
    sum2(3)
    sum3(1)
    sum1(5)
    sum2(4)
    sum4(0)
    back = small_grads()
    sum4(2)
    sum3(3)
    sum2(5)
    sum4(1)
    input_grad(0)
    sum1(6)
    sum5(0)
    input_grad(1)
    sum3(5)
    sum3(4)
    sum2(6)
    sum5(2)
    sum4(3)
    sum5(1)
    sum4(5)
    sum3(6)
    sum6(0)
    sum6(2)
    sum4(4)
    sum6(1)
    sum5(3)
    input_grad(2)
    input_grad(3)
    sum4(6)
    sum5(5)
    input_grad(4)
    sum6(3)
    sum7(0)
    sum5(4)
    sum7(1)
    input_grad(5)
    sum5(6)
    input_grad(6)
    sum6(5)
    input_grad(7)
    sum6(4)
    sum6(6)
    sum7(2)
    sum7(5)
    sum7(3)
    collect()
    sum7(4)
    sum7(6)

    @pl.loop(1, 16)
    def _(o):
        t = (s + o) % 16
        map_copy(o).wait_send()
        links.copy(
            gx.at[pl.ds(0, ROWS)], gx.at[pl.ds(0, ROWS)], gx_s.at[t], gx_s.at[t], dp, t
        ).wait_send()

    proj_forward(0).wait_send()

    @pl.loop(1, 8)
    def _(o):
        proj_copy(o).wait_send()
        proj_forward(o).wait_send()
        note_copy(0, o).wait_send()
        note_copy(1, o).wait_send()
        proj_grad_copy(o).wait_send()

    own_maps().wait()
    own_head().wait()
    for p in range(7):
        store(p).wait()
    links.flush()


def finish_kernel(
    head_in, d_in, d3_in, maps_in, head_out, maps_out, atrous, point, pool, bias, proj, proj_bias,
    d, d3, wide, wide3, maps, head, in_s, out_s,
):
    s = lax.axis_index("space")
    loads = [pltpu.make_async_copy(d3_in, d3, in_s.at[6])]
    loads += [pltpu.make_async_copy(half(d_in, i), half(d, i), in_s.at[i]) for i in range(6)]
    loads += [pltpu.make_async_copy(maps_in, maps, in_s.at[7]), pltpu.make_async_copy(head_in, head, in_s.at[8])]
    for copy in loads:
        copy.start()
    loads[0].wait()
    wide3[...] = d3[0:336].astype(f32)
    rows = d3[336:352].astype(f32)
    picked = jnp.zeros((5, 16), f32)
    for i in range(16):
        picked = jnp.where(s == i, rows[0:5, 16 * i : 16 * i + 16], picked)
    bias[...] = picked
    proj_bias[...] = rows[5:6]
    stores = [
        pltpu.make_async_copy(wide3.at[pl.ds(0, 128)], point, out_s.at[8]),
        pltpu.make_async_copy(wide3.at[pl.ds(128, 128)], pool, out_s.at[9]),
        pltpu.make_async_copy(wide3.at[pl.ds(256, 80)], proj, out_s.at[10]),
    ]
    for copy in stores:
        copy.start()
    for i in range(6):
        loads[1 + i].wait()
        k, first = i // 2, 576 * (i % 2)
        wide[k, first : first + 576] = d[k, first : first + 576].astype(f32)
        copy = pltpu.make_async_copy(half(wide, i), half(atrous, i), out_s.at[i])
        copy.start()
        stores.append(copy)
    loads[7].wait()
    loads[8].wait()
    through = [
        pltpu.make_async_copy(maps, maps_out, out_s.at[6]), pltpu.make_async_copy(head, head_out, out_s.at[7]),
    ]
    for copy in through:
        copy.start()
    for copy in stores + through:
        copy.wait()


def half(array, i):
    return array.at[i // 2, pl.ds(576 * (i % 2), 576)]


def dma(*shape):
    return pltpu.SemaphoreType.DMA(shape)


def vm(dtype, *shape):
    return pltpu.VMEM(shape, dtype)


def body(feature_maps, w_atrous, w_point, w_pool, bias_branch, w_proj, bias_proj, cotangent):
    hbm = pl.BlockSpec(memory_space=pl.ANY)
    vmem = pl.BlockSpec(memory_space=pltpu.VMEM)
    shape = jax.ShapeDtypeStruct
    results = pl.pallas_call(
        aspp_kernel,
        out_shape=(
            shape((ROWS, 256), bf16), shape((3, 1152, 256), bf16), shape((384, 256), bf16),
            shape((ROWS, 2048), bf16),
        ),
        in_specs=[hbm] * 8,
        out_specs=[hbm] * 4,
        scratch_shapes=[
            vm(bf16, ROWS, 2048), vm(bf16, 3, 1152, 256), vm(bf16, 128, 256), vm(bf16, 128, 256), vm(f32, 5, 16),
            vm(bf16, 5, 16, 256), vm(f32, 1, 256), vm(bf16, ROWS, 256),
            vm(bf16, ROWS, 256), vm(bf16, 3, 1152, 256), vm(bf16, 384, 256),
            vm(bf16, PIX, 128), vm(bf16, 3, PIX + 2 * PAD, 384),
            vm(bf16, 4, 8, ROWS, 256), vm(bf16, 4, 8, ROWS, 256), vm(f32, 4, 8, ROWS, 256),
            vm(bf16, 4, ROWS, 256), vm(bf16, 4, ROWS, 256), vm(bf16, 4, ROWS, 256), vm(bf16, 4, ROWS, 256),
            vm(bf16, 4, 2, ROWS, 256), vm(bf16, 4, 2, ROWS, 256),
            vm(bf16, 4, 2, ROWS, 256), vm(bf16, 4, 2, ROWS, 256),
            vm(bf16, 4, ROWS, 256), vm(bf16, 4, ROWS, 256), vm(bf16, 4, ROWS, 256), vm(bf16, 4, ROWS, 256),
            vm(bf16, 5, 256, 256), vm(f32, 4, ROWS, 256), vm(bf16, 4, ROWS, 256),
            vm(bf16, 3, PIX + 2 * PAD, 256), vm(bf16, PIX, 256), vm(bf16, 3, 384, PIX),
            vm(f32, 3, 1152, 256), vm(f32, 384, 256), vm(f32, 7, 4, 96, 128),
            vm(bf16, 2, 5, 8, 16, 256), vm(bf16, 5, 8, 16, 256), vm(bf16, 5, 8, 16, 256),
            vm(bf16, 8, 5, 16, 256),
            vm(f32, 2, 8, 256), vm(f32, 2, 8, 256), vm(f32, 2, 8, 256), vm(f32, 2, 8, 8, 256),
            vm(bf16, PIX, 128),
            dma(8), dma(9), dma(16), dma(16), dma(8), dma(8), dma(8), dma(8), dma(4, 6), dma(4, 6),
            dma(4, 15), dma(4, 16), dma(7, 14), dma(7, 14),
            dma(8), dma(8), dma(2, 9), dma(2, 9), dma(16), dma(16),
            *[vm(bf16, 2, h, 256) for h in HALVES], *[vm(bf16, 2, h, 256) for h in HALVES],
            *[vm(bf16, 2, 2, h, 256) for h in HALVES], *[vm(bf16, 2, 2, h, 256) for h in HALVES],
            *[vm(bf16, 4, h, 128) for h in HALVES], *[vm(bf16, 3, h, 128) for h in HALVES],
            *[vm(bf16, 4, h, 128) for h in HALVES],
        ],
        compiler_params=pltpu.CompilerParams(
            collective_id=0, has_side_effects=True, vmem_limit_bytes=VMEM_LIMIT
        ),
        name="aspp",
    )(
        feature_maps.reshape(ROWS, 2048), w_atrous.reshape(3, 1152, 256), w_point, w_pool, bias_branch,
        w_proj, bias_proj.reshape(1, 256), cotangent.reshape(ROWS, 256),
    )
    head_out, grad_maps, atrous, point, pool, bias, proj, proj_bias = pl.pallas_call(
        finish_kernel,
        out_shape=(
            shape((ROWS, 256), bf16), shape((ROWS, 2048), bf16), shape((3, 1152, 256), f32),
            shape((128, 256), f32), shape((128, 256), f32), shape((5, 16), f32), shape((80, 256), f32),
            shape((1, 256), f32),
        ),
        in_specs=[hbm] * 4,
        out_specs=[hbm] * 5 + [vmem, hbm, vmem],
        scratch_shapes=[
            vm(bf16, 3, 1152, 256), vm(bf16, 384, 256), vm(f32, 3, 1152, 256), vm(f32, 336, 256),
            vm(bf16, ROWS, 2048), vm(bf16, ROWS, 256), dma(9), dma(11),
        ],
        compiler_params=pltpu.CompilerParams(vmem_limit_bytes=VMEM_LIMIT),
        name="finish",
    )(*results)
    return (
        head_out.reshape(1, 3, 48, 256),
        grad_maps.reshape(1, 3, 48, 2048),
        atrous.reshape(3, 9, 128, 256),
        point,
        pool,
        bias,
        proj.reshape(5, 16, 256),
        proj_bias.reshape(256),
    )


def solution(mesh):
    placed = (
        P("dp", "space", None, None),
        P(None, None, "space", None),
        P("space", None),
        P("space", None),
        P(None, "space"),
        P(None, "space", None),
        P(),
        P("dp", "space", None, None),
    )
    return jax.shard_map(
        body,
        mesh=mesh,
        in_specs=placed,
        out_specs=(
            P("dp", "space", None, None),
            P("dp", "space", None, None),
            P(None, None, "space", None),
            P("space", None),
            P("space", None),
            P(None, "space"),
            P(None, "space", None),
            P(),
        ),
        check_vma=False,
    )
```

```python
import jax
import jax.numpy as jnp
from jax import lax
from jax.experimental import pallas as pl
from jax.experimental.pallas import tpu as pltpu
from jax.sharding import PartitionSpec as P

bf16 = jnp.bfloat16
f32 = jnp.float32
dilations = (6, 12, 18)
MESH = pl.DeviceIdType.MESH
ROWS = 144
PIX = 2304
PAD = 864
NT = (((1,), (1,)), ((), ()))
TN = (((0,), (0,)), ((), ()))
BLOCK = 576
VMEM_LIMIT = 60 * 2**20


def silu_slope(values):
    sigma = jax.nn.sigmoid(values)
    return sigma * (1.0 + values * (1.0 - sigma))


def dot(a, b):
    return jnp.dot(a, b, preferred_element_type=f32)


def dot_nt(a, b):
    return lax.dot_general(a, b, NT, preferred_element_type=f32)


def aligned(value, step=16):
    return value if isinstance(value, int) else pl.multiple_of(value, step)


class Links:
    def __init__(self, dp, space):
        self.dp = dp
        self.space = space
        self.sent = []

    def copy(self, src, dst, ssem, rsem, dp, space):
        return pltpu.make_async_remote_copy(
            src_ref=src, dst_ref=dst, send_sem=ssem, recv_sem=rsem, device_id=(dp, space), device_id_type=MESH
        )

    def send(self, src, dst, ssem, rsem, dp=None, space=None):
        c = self.copy(src, dst, ssem, rsem, self.dp if dp is None else dp, self.space if space is None else space)
        c.start()
        self.sent.append(c)

    def arrived(self, ref, rsem):
        self.copy(ref, ref, rsem, rsem, self.dp, self.space).wait_recv()

    def flush(self):
        for c in self.sent:
            c.wait_send()


def shifted(block, d, rows, sign):
    lanes = block.shape[1]
    v = block.reshape(rows, 48, lanes)
    col = lax.broadcasted_iota(jnp.int32, (rows, 48, lanes), 1)
    if sign < 0:
        v = jnp.where(col >= d, pltpu.roll(v, d, 1), 0.0)
    else:
        v = jnp.where(col < 48 - d, pltpu.roll(v, 48 - d, 1), 0.0)
    return v.reshape(rows * 48, lanes)


PIECES = ((0, 0, 2, 96), (0, 2, 3, 48), (1, 0, 2, 96), (1, 2, 3, 48), (2, 0, 2, 96), (2, 2, 3, 48), (3, 0, 1, 48))
HALVES = tuple(piece[3] for piece in PIECES)
CUT = 80
SMALL_BLOCK = 288


def aspp_kernel(
    maps_in, w_in, w_point_in, w_pool_in, bias_in, w_proj_in, bias_proj_in, cot_in,
    head_to, d_to, d3_to, maps_out,
    maps, w, w_point, w_pool, bias, w_proj, bias_proj, cot, head_out, d, d3,
    x, c, core_out, core_in, acc, sa, sb, ra, rb, s2p, s2m, r2p, r2m, sz, rz, zs, zin, wp, slopes, acts,
    gp, g3, xt, dw, dw3, own, gpo, gpi, gps, gpr, note, note_in, note_sum, notes, gx,
    in_s, out_s, x_s, x_r, wp_s, wp_r, wf_s, wf_r, rs_s, rs_r,
    ag_s, ag_r, ar_s, ar_r, gp_s, gp_r, note_s, note_r, gx_s, gx_r, *pieces,
):
    u1s, u1r, u2s, u2r, es, zr, zt = [pieces[7 * i : 7 * i + 7] for i in range(7)]
    dp = lax.axis_index("dp")
    s = lax.axis_index("space")
    core = s % 2
    chip = s // 2
    cx = chip % 4
    cz = chip // 4
    xp = (cx + 1) % 4
    xm = (cx + 3) % 4
    x2 = (cx + 2) % 4

    def at(z, col, half):
        return (z * 4 + col) * 2 + half

    right = at(cz, xp, core)
    left = at(cz, xm, core)
    other_z = at(1 - cz, cx, core)
    sibling = at(cz, cx, 1 - core)
    y = dp % 4
    hz = dp // 4
    yp = (y + 1) % 4
    ym = (y + 3) % 4
    y2 = (y + 2) % 4
    up = hz * 4 + yp
    down = hz * 4 + ym
    links = Links(dp, s)

    loads = [
        pltpu.make_async_copy(source, target, in_s.at[i])
        for i, (source, target) in enumerate((
            (maps_in, maps), (w_proj_in, w_proj), (w_point_in, w_point), (w_pool_in, w_pool), (bias_in, bias),
            (bias_proj_in, bias_proj), (cot_in, cot), (w_in, w),
        ))
    ]
    for load in loads:
        load.start()
    barrier = pltpu.get_barrier_semaphore()

    @pl.loop(1, 16)
    def _(o):
        pl.semaphore_signal(barrier, inc=1, device_id=(dp, (s + o) % 16), device_id_type=MESH)

    pl.semaphore_signal(barrier, inc=1, device_id=(up, s), device_id_type=MESH)
    pl.semaphore_signal(barrier, inc=1, device_id=(down, s), device_id_type=MESH)
    for o in range(1, 4):
        pl.semaphore_signal(barrier, inc=1, device_id=(((hz + o) % 4) * 4 + y, s), device_id_type=MESH)
    pl.semaphore_wait(barrier, 20)

    def map_copy(o):
        t = (s + o) % 16
        return links.copy(
            maps.at[:, pl.ds(aligned(t * 128, 128), 128)], x.at[pl.ds(aligned(s * ROWS), ROWS)],
            x_s.at[o], x_r.at[o], dp, t,
        )

    loads[0].wait()

    @pl.loop(1, 16)
    def _(o):
        map_copy(o).start()

    for load in loads[1:7]:
        load.wait()

    x[pl.ds(aligned(s * ROWS), ROWS)] = maps[:, pl.ds(aligned(s * 128, 128), 128)]
    wp[:, pl.ds(aligned(s * 16), 16)] = w_proj[...]
    for k in range(3):
        c[k, 0:PAD] = jnp.zeros((PAD, 384), bf16)
        c[k, PAD + PIX : PAD + PIX + PAD] = jnp.zeros((PAD, 384), bf16)
        gp[k, 0:PAD] = jnp.zeros((PAD, 256), bf16)
        gp[k, PAD + PIX : PAD + PIX + PAD] = jnp.zeros((PAD, 256), bf16)

    def build(o, total):
        t = (s + 16 - o) % 16
        base = aligned(t * ROWS)
        raw = x[pl.ds(base, ROWS)]
        v = raw.astype(f32)
        for k, d in enumerate(dilations):
            lo = shifted(v, d, 3, -1).astype(bf16)
            hi = shifted(v, d, 3, 1).astype(bf16)
            c[k, pl.ds(aligned(PAD + base), ROWS)] = jnp.concatenate([lo, raw, hi], axis=1)
        return total + jnp.sum(v.reshape(18, 8, 128), axis=0)

    total = build(0, jnp.zeros((8, 128), f32))

    def build_remote(o, total):
        t = (s + 16 - o) % 16
        links.arrived(x.at[pl.ds(aligned(t * ROWS), ROWS)], x_r.at[o])
        return build(o, total)

    total = lax.fori_loop(1, 16, build_remote, total)

    def proj_part(t):
        return wp.at[:, pl.ds(aligned(t * 16), 16)]

    def proj_copy(o):
        t = ((chip + o) % 8) * 2 + core
        return links.copy(proj_part(s), proj_part(s), wp_s.at[o], wp_r.at[o], dp, t)

    def proj_forward(o):
        t = ((chip + 8 - o) % 8) * 2 + core
        return links.copy(proj_part(t), proj_part(t), wf_s.at[o], wf_r.at[o], dp, sibling)

    @pl.loop(1, 8)
    def _(o):
        proj_copy(o).start()

    proj_forward(0).start()

    def note_first(n):
        links.send(note.at[n], note_in.at[n], note_s.at[n, 8], note_r.at[n, 8], space=sibling)

    def note_copy(n, o):
        t = ((chip + o) % 8) * 2 + core
        return links.copy(note_sum.at[n], notes.at[n, chip], note_s.at[n, o], note_r.at[n, o], dp, t)

    def note_second(n):
        links.arrived(note_in.at[n], note_r.at[n, 8])
        note_sum[n] = note[n] + note_in[n]
        notes[n, pl.ds(chip, 1)] = note_sum[n][None]

        @pl.loop(1, 8)
        def _(o):
            note_copy(n, o).start()

    def note_total(n):
        @pl.loop(1, 8)
        def _(o):
            links.arrived(notes.at[n, (chip + 8 - o) % 8], note_r.at[n, o])

        return lax.fori_loop(0, 8, lambda i, v: v + notes[n, i], jnp.zeros((8, 256), f32))

    def respond(k, lo, hi):
        @pl.loop(lo, hi)
        def _(i):
            base = aligned(i * BLOCK)
            if k < 3:
                d = dilations[k] * 48
                lhs = jnp.concatenate(
                    [c[k, pl.ds(aligned(PAD + base + (a - 1) * d), BLOCK)] for a in range(3)], axis=1
                )
                p = dot(lhs, w[k])
            else:
                p = dot(c[0, pl.ds(aligned(PAD + base), BLOCK), 128:256], w_point[...])
            p = p.reshape(2, 2, ROWS, 256)
            first = core == 0
            acc[k, pl.ds(i * 2, 2)] = jnp.where(first, p[:, 0], p[:, 1])
            core_out[k, pl.ds(i * 2, 2)] = jnp.where(first, p[:, 1], p[:, 0]).astype(bf16)

        if hi == PIX // BLOCK:
            links.send(core_out.at[k], core_in.at[k], rs_s.at[k, 0], rs_r.at[k, 0], space=sibling)

    def step1(k):
        links.arrived(core_in.at[k], rs_r.at[k, 0])

        @pl.loop(0, 8)
        def _(j):
            acc[k, j] = acc[k, j] + core_in[k, j].astype(f32)

        sa[k] = acc[k, x2].astype(bf16)
        links.send(sa.at[k], ra.at[k], rs_s.at[k, 1], rs_r.at[k, 1], space=right)
        sb[k] = acc[k, 4 + x2].astype(bf16)
        links.send(sb.at[k], rb.at[k], rs_s.at[k, 2], rs_r.at[k, 2], space=left)

    def cross1(k):
        links.arrived(core_in.at[k], rs_r.at[k, 0])

        @pl.loop(0, 8)
        def _(j):
            acc[k, j] = acc[k, j] + core_in[k, j].astype(f32)

        @pl.loop(0, 4)
        def _(j):
            zs[j] = acc[k, (1 - cz) * 4 + j].astype(bf16)

        links.send(zs, zin, rs_s.at[k, 1], rs_r.at[k, 1], space=other_z)

    def cross2(k):
        links.arrived(zin, rs_r.at[k, 1])

        @pl.loop(0, 4)
        def _(j):
            acc[k, cz * 4 + j] = acc[k, cz * 4 + j] + zin[j].astype(f32)

        sa[k] = acc[k, cz * 4 + x2].astype(bf16)
        upper, lower = pl.ds(0, CUT), pl.ds(CUT, ROWS - CUT)
        links.send(sa.at[k, upper], ra.at[k, upper], rs_s.at[k, 2], rs_r.at[k, 2], space=right)
        links.send(sa.at[k, lower], ra.at[k, lower], rs_s.at[k, 3], rs_r.at[k, 3], space=left)

    def cross3(k):
        links.arrived(ra.at[k, pl.ds(0, CUT)], rs_r.at[k, 2])
        s2p[k, 0, 0:CUT] = (acc[k, cz * 4 + xp, 0:CUT] + ra[k, 0:CUT].astype(f32)).astype(bf16)
        s2p[k, 0, CUT:ROWS] = acc[k, cz * 4 + xp, CUT:ROWS].astype(bf16)
        links.send(s2p.at[k, 0], r2p.at[k, 0], rs_s.at[k, 4], rs_r.at[k, 4], space=right)
        links.arrived(ra.at[k, pl.ds(CUT, ROWS - CUT)], rs_r.at[k, 3])
        s2m[k, 0, 0:CUT] = acc[k, cz * 4 + xm, 0:CUT].astype(bf16)
        s2m[k, 0, CUT:ROWS] = (acc[k, cz * 4 + xm, CUT:ROWS] + ra[k, CUT:ROWS].astype(f32)).astype(bf16)
        links.send(s2m.at[k, 0], r2m.at[k, 0], rs_s.at[k, 5], rs_r.at[k, 5], space=left)

    def cross4(k):
        links.arrived(r2p.at[k, 0], rs_r.at[k, 4])
        links.arrived(r2m.at[k, 0], rs_r.at[k, 5])
        return acc[k, cz * 4 + cx] + (r2p[k, 0].astype(f32) + r2m[k, 0].astype(f32))

    def step2(k):
        links.arrived(ra.at[k], rs_r.at[k, 1])
        s2p[k, 0] = (acc[k, xp] + ra[k].astype(f32)).astype(bf16)
        s2p[k, 1] = acc[k, 4 + xp].astype(bf16)
        links.send(s2p.at[k], r2p.at[k], rs_s.at[k, 3], rs_r.at[k, 3], space=right)
        links.arrived(rb.at[k], rs_r.at[k, 2])
        s2m[k, 0] = acc[k, xm].astype(bf16)
        s2m[k, 1] = (acc[k, 4 + xm] + rb[k].astype(f32)).astype(bf16)
        links.send(s2m.at[k], r2m.at[k], rs_s.at[k, 4], rs_r.at[k, 4], space=left)

    def step3(k):
        links.arrived(r2p.at[k], rs_r.at[k, 3])
        links.arrived(r2m.at[k], rs_r.at[k, 4])
        for z in range(2):
            acc[k, z * 4 + cx] = acc[k, z * 4 + cx] + (r2p[k, z].astype(f32) + r2m[k, z].astype(f32))
        sz[k] = acc[k, (1 - cz) * 4 + cx].astype(bf16)
        links.send(sz.at[k], rz.at[k], rs_s.at[k, 5], rs_r.at[k, 5], space=other_z)

    def step4(k):
        links.arrived(rz.at[k], rs_r.at[k, 5])
        return acc[k, cz * 4 + cx] + rz[k].astype(f32)

    def turn(lo, hi):
        @pl.loop(lo, hi)
        def _(i):
            st = aligned(i * 384, 128)
            v = x[pl.ds(st, 384)].astype(f32)
            mid = jnp.transpose(v).astype(bf16)
            for k, d in enumerate(dilations):
                xt[k, 0:128, pl.ds(st, 384)] = jnp.transpose(shifted(v, d, 8, -1)).astype(bf16)
                xt[k, 128:256, pl.ds(st, 384)] = mid
                xt[k, 256:384, pl.ds(st, 384)] = jnp.transpose(shifted(v, d, 8, 1)).astype(bf16)

    respond(3, 0, 4)

    pooled = (jnp.sum(total, axis=0, keepdims=True) / PIX).astype(bf16)
    pooled = jnp.broadcast_to(pooled, (16, 128))
    pool_part = dot(pooled, w_pool[...])[0:8]
    note[0] = jnp.zeros((8, 256), f32)
    for i in range(16):
        note[0, 1:6, 16 * i : 16 * i + 16] = bias[...]
    row = lax.broadcasted_iota(jnp.int32, (8, 256), 0)
    lane = lax.broadcasted_iota(jnp.int32, (8, 256), 1)
    mine = (lane >= s * 16) & (lane < s * 16 + 16)
    note[0] = jnp.where(row == 0, pool_part, jnp.where(mine, note[0], 0.0))
    note_first(0)

    loads[7].wait()
    respond(0, 0, 2)
    step1(3)
    note_second(0)
    respond(0, 2, 4)
    respond(1, 0, 2)
    step1(0)
    step2(3)
    respond(1, 2, 4)

    @pl.loop(1, 8)
    def _(o):
        links.arrived(proj_part(((chip + 8 - o) % 8) * 2 + core), wp_r.at[o])
        proj_forward(o).start()

    respond(2, 0, 2)
    cross1(1)
    step2(0)
    step3(3)
    respond(2, 2, 4)
    turn(0, 2)
    step1(2)
    turn(2, 4)
    cross2(1)
    step3(0)
    step2(2)

    @pl.loop(0, 8)
    def _(o):
        links.arrived(proj_part(((chip + 8 - o) % 8) * 2 + 1 - core), wf_r.at[o])

    head_note = note_total(0)
    pool_pre = head_note[0:1] + head_note[5:6]
    pool_act = jnp.broadcast_to(jax.nn.silu(pool_pre).astype(bf16).astype(f32), (ROWS, 256)).astype(bf16)

    def absorb(k):
        pre = (cross4(k) if k == 1 else step4(k)) + head_note[1 + k : 2 + k]
        sigma = jax.nn.sigmoid(pre)
        slopes[k] = sigma * (1.0 + pre * (1.0 - sigma))
        act = (pre * sigma).astype(bf16)
        acts[k] = act
        return dot(act, wp[k])

    head = bias_proj[...] + dot(pool_act, wp[4])
    head = head + absorb(3)
    turn(4, 6)
    cross3(1)
    step3(2)
    head = head + absorb(0)
    head = head + absorb(1)
    head = head + absorb(2)
    sigma = jax.nn.sigmoid(head)
    grad_f = cot[...].astype(f32) * (sigma * (1.0 + head * (1.0 - sigma)))
    grad = grad_f.astype(bf16)

    def block(k, n):
        if k < 3:
            return gp.at[k, pl.ds(aligned(PAD + n * ROWS), ROWS)]
        return g3.at[pl.ds(aligned(n * ROWS), ROWS)]

    def pass_on(k, n, slot, to):
        b = block(k, n)
        links.send(b, b, ag_s.at[k, slot], ag_r.at[k, n], space=to)

    def have(k, n):
        links.arrived(block(k, n), ag_r.at[k, n])

    def own_block(k):
        g = (dot_nt(grad, wp[k]) * slopes[k]).astype(bf16)
        if k < 3:
            gp[k, pl.ds(aligned(PAD + s * ROWS), ROWS)] = g
        else:
            g3[pl.ds(aligned(s * ROWS), ROWS)] = g
        pass_on(k, s, 0, other_z)
        pass_on(k, s, 1, right)
        pass_on(k, s, 2, left)
        pass_on(k, s, 3, sibling)
        note[1, k : k + 1] = jnp.sum(g.astype(f32), axis=0, keepdims=True)

    def head_store():
        head_out[...] = (head * sigma).astype(bf16)
        own_head().start()

    def gather1(k):
        n = at(1 - cz, cx, core)
        have(k, n)
        pass_on(k, n, 4, right)
        pass_on(k, n, 5, left)
        pass_on(k, n, 6, sibling)

    def gather2(k):
        n = at(0, xm, core)
        have(k, n)
        pass_on(k, n, 7, right)
        pass_on(k, n, 8, sibling)
        n = at(1, xp, core)
        have(k, n)
        pass_on(k, n, 9, left)
        pass_on(k, n, 10, sibling)
        n = at(1, xm, core)
        have(k, n)
        pass_on(k, n, 11, sibling)
        n = at(0, xp, core)
        have(k, n)
        pass_on(k, n, 12, sibling)

    def gather3(k):
        for z in range(2):
            n = at(z, x2, core)
            have(k, n)
            pass_on(k, n, 13 + z, sibling)

    def gather4(k):
        for z in range(2):
            for col in (cx, xp, xm, x2):
                have(k, at(z, col, 1 - core))

    def proj_grad():
        for k in range(5):
            act = acts[k] if k < 4 else pool_act
            g = lax.dot_general(act, grad, TN, preferred_element_type=f32).astype(bf16)
            g = g.reshape(8, 2, 16, 256)
            gpo[0, k] = g[:, 0]
            gpo[1, k] = g[:, 1]
        links.send(gpo.at[1 - core], gpi, gp_s.at[0], gp_r.at[0], space=sibling)

    def note_start():
        note[1, 4:5] = jnp.sum(dot_nt(grad, wp[4]), axis=0, keepdims=True)
        note[1, 5:6] = jnp.sum(grad.astype(f32), axis=0, keepdims=True)
        note[1, 6:8] = jnp.zeros((2, 256), f32)
        note_first(1)

    def weight_grad(p):
        k, first, last, _ = PIECES[p]
        d = 48 * dilations[k]
        for a, (lo, hi) in enumerate(
            ((0, -((d - PIX) // 128) * 128), (0, PIX), (d // 128 * 128, PIX))
        ):
            if first <= a < last:
                g0 = PAD + lo - (a - 1) * d
                dw[k, 384 * a : 384 * (a + 1)] = dot(xt[k, :, lo:hi], gp[k, g0 : g0 + hi - lo])

    def summed(p, start, size):
        k, first, _, _ = PIECES[p]
        if k == 3:
            return dw3[pl.ds(aligned(start), size)]
        return dw[k, pl.ds(aligned(384 * first + start), size)]

    def result(p, start, size):
        k, first, _, _ = PIECES[p]
        if k == 3:
            return d3.at[pl.ds(aligned(start), size)]
        return d.at[k, pl.ds(aligned(384 * first + start), size)]

    def sum1(k):
        h = HALVES[k]
        u1s[k][0] = summed(k, y2 * 2 * h, h).astype(bf16)
        links.send(u1s[k].at[0], u1r[k].at[0], ar_s.at[k, 0], ar_r.at[k, 0], dp=up)
        u1s[k][1] = summed(k, y2 * 2 * h + h, h).astype(bf16)
        links.send(u1s[k].at[1], u1r[k].at[1], ar_s.at[k, 1], ar_r.at[k, 1], dp=down)

    def sum2(k):
        h = HALVES[k]
        links.arrived(u1r[k].at[0], ar_r.at[k, 0])
        u2s[k][0, 0] = (summed(k, yp * 2 * h, h) + u1r[k][0].astype(f32)).astype(bf16)
        u2s[k][0, 1] = summed(k, yp * 2 * h + h, h).astype(bf16)
        links.send(u2s[k].at[0], u2r[k].at[0], ar_s.at[k, 2], ar_r.at[k, 2], dp=up)
        links.arrived(u1r[k].at[1], ar_r.at[k, 1])
        u2s[k][1, 0] = summed(k, ym * 2 * h, h).astype(bf16)
        u2s[k][1, 1] = (summed(k, ym * 2 * h + h, h) + u1r[k][1].astype(f32)).astype(bf16)
        links.send(u2s[k].at[1], u2r[k].at[1], ar_s.at[k, 3], ar_r.at[k, 3], dp=down)

    def sum3(k):
        h = HALVES[k]
        links.arrived(u2r[k].at[0], ar_r.at[k, 2])
        links.arrived(u2r[k].at[1], ar_r.at[k, 3])
        for half in range(2):
            v = summed(k, y * 2 * h + half * h, h) + (
                u2r[k][0, half].astype(f32) + u2r[k][1, half].astype(f32)
            )
            for lanes in range(2):
                quarter = v[:, 128 * lanes : 128 * (lanes + 1)]
                own[k, 2 * half + lanes, 0:h] = quarter
                es[k][2 * half + lanes] = quarter.astype(bf16)
        for o in range(1, 4):
            q = (hz + o) % 4
            links.send(es[k].at[q], zr[k].at[o - 1], ar_s.at[k, 3 + o], ar_r.at[k, 3 + o], dp=q * 4 + y)

    def sum4(k):
        h = HALVES[k]
        v = own[k, hz, 0:h]
        for o in range(1, 4):
            links.arrived(zr[k].at[o - 1], ar_r.at[k, 3 + o])
            v = v + zr[k][o - 1].astype(f32)
        zt[k][hz] = v.astype(bf16)
        for o in range(1, 4):
            q = (hz + o) % 4
            links.send(zt[k].at[hz], zt[k].at[hz], ar_s.at[k, 6 + o], ar_r.at[k, 6 + o], dp=q * 4 + y)

    def chunk(k, n):
        h = HALVES[k]
        return result(k, n * 2 * h, 2 * h)

    def half_chunk(k, n, half):
        h = HALVES[k]
        return result(k, n * 2 * h + half * h, h)

    def sum5(k):
        h = HALVES[k]
        for o in range(1, 4):
            links.arrived(zt[k].at[(hz + 4 - o) % 4], ar_r.at[k, 6 + o])
        for half in range(2):
            result(k, y * 2 * h + half * h, h)[...] = jnp.concatenate(
                [zt[k][2 * half], zt[k][2 * half + 1]], axis=1
            )
        share = chunk(k, y)
        links.send(share, share, ar_s.at[k, 10], ar_r.at[k, 10], dp=up)
        links.send(share, share, ar_s.at[k, 11], ar_r.at[k, 11], dp=down)

    def sum6(k):
        links.arrived(chunk(k, ym), ar_r.at[k, 10])
        b = half_chunk(k, ym, 0)
        links.send(b, b, ar_s.at[k, 12], ar_r.at[k, 12], dp=up)
        links.arrived(chunk(k, yp), ar_r.at[k, 11])
        b = half_chunk(k, yp, 1)
        links.send(b, b, ar_s.at[k, 13], ar_r.at[k, 13], dp=down)

    def store(p):
        k, first, last, _ = PIECES[p]
        if k == 3:
            return pltpu.make_async_copy(d3, d3_to, out_s.at[p])
        rows = pl.ds(384 * first, 384 * (last - first))
        return pltpu.make_async_copy(d.at[k, rows], d_to.at[k, rows], out_s.at[p])

    def sum7(k):
        links.arrived(half_chunk(k, y2, 0), ar_r.at[k, 12])
        links.arrived(half_chunk(k, y2, 1), ar_r.at[k, 13])
        store(k).start()

    def proj_grad_copy(o):
        j = (chip + o) % 8
        return links.copy(gps.at[:, j], gpr.at[chip], gp_s.at[o], gp_r.at[o], dp, j * 2 + core)

    def proj_grad_share():
        links.arrived(gpi, gp_r.at[0])
        gps[...] = (gpo[core].astype(f32) + gpi[...].astype(f32)).astype(bf16)

        @pl.loop(1, 8)
        def _(o):
            proj_grad_copy(o).start()

    def small_grads():
        dw3[0:128] = dot(xt[0, 128:256, :], g3[...])
        totals = note_total(1)
        pool_grad = (silu_slope(pool_pre) * totals[4:5]).astype(bf16)
        pool_row = pool_grad.astype(f32)
        column = jnp.transpose(jnp.broadcast_to(pooled[0:1].astype(f32), (128, 128)))
        dw3[128:256] = jnp.concatenate([column, column], axis=1) * pool_row

        @pl.loop(1, 8)
        def _(o):
            links.arrived(gpr.at[(chip + 8 - o) % 8], gp_r.at[o])

        gpr[pl.ds(chip, 1)] = gps[:, pl.ds(chip, 1)].reshape(1, 5, 16, 256)
        dw3[256:336] = lax.fori_loop(
            0, 8, lambda i, v: v + gpr[i].astype(f32).reshape(80, 256), jnp.zeros((80, 256), f32)
        )
        dw3[336:384] = jnp.zeros((48, 256), f32)
        dw3[336:340] = totals[0:4]
        dw3[340:341] = pool_row
        dw3[341:342] = totals[5:6]
        return dot_nt(jnp.broadcast_to(pool_row, (16, 256)).astype(bf16), w_pool[...])[0:1] / PIX

    def input_grad(i):
        size = SMALL_BLOCK
        st = i * size
        total = dot_nt(g3[st : st + size], w_point[...]) + back
        for k in range(3):
            d = 48 * dilations[k]
            sides = 0.0
            for a in range(3):
                g0 = PAD + st - (a - 1) * d
                g = gp[k, g0 : g0 + size]
                tap = 384 * a
                ends = jnp.concatenate([w[k, tap : tap + 128], w[k, tap + 256 : tap + 384]], axis=0)
                sides = sides + dot_nt(g, ends)
                total = total + dot_nt(g, w[k, tap + 128 : tap + 256])
            total = total + shifted(sides[:, 0:128], dilations[k], size // 48, 1)
            total = total + shifted(sides[:, 128:256], dilations[k], size // 48, -1)
        gx[st : st + size] = total.astype(bf16)
        for j in range(size // ROWS):
            n = i * (size // ROWS) + j

            @pl.when(s != n)
            def _():
                gx_copy(n).start()

    def gx_copy(n):
        return links.copy(
            gx.at[pl.ds(n * ROWS, ROWS)], maps_out.at[:, pl.ds(aligned(s * 128, 128), 128)],
            gx_s.at[n], gx_r.at[s], dp, n,
        )

    def own_maps():
        return pltpu.make_async_copy(
            gx.at[pl.ds(aligned(s * ROWS), ROWS)], maps_out.at[:, pl.ds(aligned(s * 128, 128), 128)], out_s.at[7]
        )

    def own_head():
        return pltpu.make_async_copy(head_out, head_to, out_s.at[8])

    def collect():
        own_maps().start()

        @pl.loop(1, 16)
        def _(o):
            t = (s + o) % 16
            links.arrived(maps_out.at[:, pl.ds(aligned(t * 128, 128), 128)], gx_r.at[t])

    own_block(1)
    own_block(2)
    own_block(0)
    proj_grad()
    head_store()
    gather1(1)
    gather1(2)
    gather1(0)
    gather2(1)
    own_block(3)
    gather2(2)
    note_start()
    gather2(0)
    gather3(1)
    gather4(1)
    weight_grad(2)
    sum1(2)
    gather3(2)
    gather1(3)
    proj_grad_share()
    weight_grad(3)
    gather4(2)
    sum1(3)
    weight_grad(5)
    sum1(5)
    gather3(0)
    sum2(2)
    weight_grad(4)
    sum1(4)
    sum2(3)
    gather4(0)
    sum2(5)
    gather2(3)
    weight_grad(1)
    sum1(1)
    note_second(1)
    sum3(2)
    sum2(4)
    weight_grad(0)
    sum1(0)
    sum3(5)
    sum3(3)
    sum2(1)
    sum4(2)
    gather3(3)
    sum3(4)
    sum2(0)
    gather4(3)
    back = small_grads()
    sum3(1)
    sum4(3)
    sum1(6)
    input_grad(0)
    sum5(2)
    sum3(0)
    sum2(6)
    sum4(1)
    sum4(4)
    sum6(2)
    sum5(3)
    sum3(6)
    sum4(5)
    sum4(0)
    input_grad(1)
    sum5(1)
    sum5(4)
    sum7(2)
    sum6(3)
    sum4(6)
    input_grad(2)
    sum5(5)
    input_grad(3)
    sum6(1)
    sum5(0)
    input_grad(4)
    input_grad(5)
    sum5(6)
    sum6(4)
    sum6(5)
    input_grad(6)
    input_grad(7)
    sum6(0)
    sum6(6)
    sum7(5)
    sum7(4)
    collect()
    sum7(1)
    sum7(0)
    sum7(3)
    sum7(6)

    @pl.loop(1, 16)
    def _(o):
        t = (s + o) % 16
        map_copy(o).wait_send()
        links.copy(
            gx.at[pl.ds(0, ROWS)], gx.at[pl.ds(0, ROWS)], gx_s.at[t], gx_s.at[t], dp, t
        ).wait_send()

    proj_forward(0).wait_send()

    @pl.loop(1, 8)
    def _(o):
        proj_copy(o).wait_send()
        proj_forward(o).wait_send()
        note_copy(0, o).wait_send()
        note_copy(1, o).wait_send()
        proj_grad_copy(o).wait_send()

    own_maps().wait()
    own_head().wait()
    for p in range(7):
        store(p).wait()
    links.flush()


def finish_kernel(
    head_in, d_in, d3_in, maps_in, head_out, maps_out, atrous, point, pool, bias, proj, proj_bias,
    d, d3, wide, wide3, maps, head, in_s, out_s,
):
    s = lax.axis_index("space")
    loads = [pltpu.make_async_copy(d3_in, d3, in_s.at[6])]
    loads += [pltpu.make_async_copy(half(d_in, i), half(d, i), in_s.at[i]) for i in range(6)]
    loads += [pltpu.make_async_copy(maps_in, maps, in_s.at[7]), pltpu.make_async_copy(head_in, head, in_s.at[8])]
    for copy in loads:
        copy.start()
    loads[0].wait()
    wide3[...] = d3[0:336].astype(f32)
    rows = d3[336:352].astype(f32)
    picked = jnp.zeros((5, 16), f32)
    for i in range(16):
        picked = jnp.where(s == i, rows[0:5, 16 * i : 16 * i + 16], picked)
    bias[...] = picked
    proj_bias[...] = rows[5:6]
    stores = [
        pltpu.make_async_copy(wide3.at[pl.ds(0, 128)], point, out_s.at[8]),
        pltpu.make_async_copy(wide3.at[pl.ds(128, 128)], pool, out_s.at[9]),
        pltpu.make_async_copy(wide3.at[pl.ds(256, 80)], proj, out_s.at[10]),
    ]
    for copy in stores:
        copy.start()
    for i in range(6):
        loads[1 + i].wait()
        k, first = i // 2, 576 * (i % 2)
        wide[k, first : first + 576] = d[k, first : first + 576].astype(f32)
        copy = pltpu.make_async_copy(half(wide, i), half(atrous, i), out_s.at[i])
        copy.start()
        stores.append(copy)
    loads[7].wait()
    loads[8].wait()
    through = [
        pltpu.make_async_copy(maps, maps_out, out_s.at[6]), pltpu.make_async_copy(head, head_out, out_s.at[7]),
    ]
    for copy in through:
        copy.start()
    for copy in stores + through:
        copy.wait()


def half(array, i):
    return array.at[i // 2, pl.ds(576 * (i % 2), 576)]


def dma(*shape):
    return pltpu.SemaphoreType.DMA(shape)


def vm(dtype, *shape):
    return pltpu.VMEM(shape, dtype)


def body(feature_maps, w_atrous, w_point, w_pool, bias_branch, w_proj, bias_proj, cotangent):
    hbm = pl.BlockSpec(memory_space=pl.ANY)
    vmem = pl.BlockSpec(memory_space=pltpu.VMEM)
    shape = jax.ShapeDtypeStruct
    results = pl.pallas_call(
        aspp_kernel,
        out_shape=(
            shape((ROWS, 256), bf16), shape((3, 1152, 256), bf16), shape((384, 256), bf16),
            shape((ROWS, 2048), bf16),
        ),
        in_specs=[hbm] * 8,
        out_specs=[hbm] * 4,
        scratch_shapes=[
            vm(bf16, ROWS, 2048), vm(bf16, 3, 1152, 256), vm(bf16, 128, 256), vm(bf16, 128, 256), vm(f32, 5, 16),
            vm(bf16, 5, 16, 256), vm(f32, 1, 256), vm(bf16, ROWS, 256),
            vm(bf16, ROWS, 256), vm(bf16, 3, 1152, 256), vm(bf16, 384, 256),
            vm(bf16, PIX, 128), vm(bf16, 3, PIX + 2 * PAD, 384),
            vm(bf16, 4, 8, ROWS, 256), vm(bf16, 4, 8, ROWS, 256), vm(f32, 4, 8, ROWS, 256),
            vm(bf16, 4, ROWS, 256), vm(bf16, 4, ROWS, 256), vm(bf16, 4, ROWS, 256), vm(bf16, 4, ROWS, 256),
            vm(bf16, 4, 2, ROWS, 256), vm(bf16, 4, 2, ROWS, 256),
            vm(bf16, 4, 2, ROWS, 256), vm(bf16, 4, 2, ROWS, 256),
            vm(bf16, 4, ROWS, 256), vm(bf16, 4, ROWS, 256), vm(bf16, 4, ROWS, 256), vm(bf16, 4, ROWS, 256),
            vm(bf16, 5, 256, 256), vm(f32, 4, ROWS, 256), vm(bf16, 4, ROWS, 256),
            vm(bf16, 3, PIX + 2 * PAD, 256), vm(bf16, PIX, 256), vm(bf16, 3, 384, PIX),
            vm(f32, 3, 1152, 256), vm(f32, 384, 256), vm(f32, 7, 4, 96, 128),
            vm(bf16, 2, 5, 8, 16, 256), vm(bf16, 5, 8, 16, 256), vm(bf16, 5, 8, 16, 256),
            vm(bf16, 8, 5, 16, 256),
            vm(f32, 2, 8, 256), vm(f32, 2, 8, 256), vm(f32, 2, 8, 256), vm(f32, 2, 8, 8, 256),
            vm(bf16, PIX, 128),
            dma(8), dma(9), dma(16), dma(16), dma(8), dma(8), dma(8), dma(8), dma(4, 6), dma(4, 6),
            dma(4, 15), dma(4, 16), dma(7, 14), dma(7, 14),
            dma(8), dma(8), dma(2, 9), dma(2, 9), dma(16), dma(16),
            *[vm(bf16, 2, h, 256) for h in HALVES], *[vm(bf16, 2, h, 256) for h in HALVES],
            *[vm(bf16, 2, 2, h, 256) for h in HALVES], *[vm(bf16, 2, 2, h, 256) for h in HALVES],
            *[vm(bf16, 4, h, 128) for h in HALVES], *[vm(bf16, 3, h, 128) for h in HALVES],
            *[vm(bf16, 4, h, 128) for h in HALVES],
        ],
        compiler_params=pltpu.CompilerParams(
            collective_id=0, has_side_effects=True, vmem_limit_bytes=VMEM_LIMIT
        ),
        name="aspp",
    )(
        feature_maps.reshape(ROWS, 2048), w_atrous.reshape(3, 1152, 256), w_point, w_pool, bias_branch,
        w_proj, bias_proj.reshape(1, 256), cotangent.reshape(ROWS, 256),
    )
    head_out, grad_maps, atrous, point, pool, bias, proj, proj_bias = pl.pallas_call(
        finish_kernel,
        out_shape=(
            shape((ROWS, 256), bf16), shape((ROWS, 2048), bf16), shape((3, 1152, 256), f32),
            shape((128, 256), f32), shape((128, 256), f32), shape((5, 16), f32), shape((80, 256), f32),
            shape((1, 256), f32),
        ),
        in_specs=[hbm] * 4,
        out_specs=[hbm] * 5 + [vmem, hbm, vmem],
        scratch_shapes=[
            vm(bf16, 3, 1152, 256), vm(bf16, 384, 256), vm(f32, 3, 1152, 256), vm(f32, 336, 256),
            vm(bf16, ROWS, 2048), vm(bf16, ROWS, 256), dma(9), dma(11),
        ],
        compiler_params=pltpu.CompilerParams(vmem_limit_bytes=VMEM_LIMIT),
        name="finish",
    )(*results)
    return (
        head_out.reshape(1, 3, 48, 256),
        grad_maps.reshape(1, 3, 48, 2048),
        atrous.reshape(3, 9, 128, 256),
        point,
        pool,
        bias,
        proj.reshape(5, 16, 256),
        proj_bias.reshape(256),
    )


def solution(mesh):
    placed = (
        P("dp", "space", None, None),
        P(None, None, "space", None),
        P("space", None),
        P("space", None),
        P(None, "space"),
        P(None, "space", None),
        P(),
        P("dp", "space", None, None),
    )
    return jax.shard_map(
        body,
        mesh=mesh,
        in_specs=placed,
        out_specs=(
            P("dp", "space", None, None),
            P("dp", "space", None, None),
            P(None, None, "space", None),
            P("space", None),
            P("space", None),
            P(None, "space"),
            P(None, "space", None),
            P(),
        ),
        check_vma=False,
    )
```

```python
import jax
import jax.numpy as jnp
from jax import lax
from jax.experimental import pallas as pl
from jax.experimental.pallas import tpu as pltpu
from jax.sharding import PartitionSpec as P

bf16 = jnp.bfloat16
f32 = jnp.float32
dilations = (6, 12, 18)
MESH = pl.DeviceIdType.MESH
ROWS = 144
PIX = 2304
PAD = 864
NT = (((1,), (1,)), ((), ()))
TN = (((0,), (0,)), ((), ()))
BLOCK = 576
VMEM_LIMIT = 60 * 2**20


def silu_slope(values):
    sigma = jax.nn.sigmoid(values)
    return sigma * (1.0 + values * (1.0 - sigma))


def dot(a, b):
    return jnp.dot(a, b, preferred_element_type=f32)


def dot_nt(a, b):
    return lax.dot_general(a, b, NT, preferred_element_type=f32)


def aligned(value, step=16):
    return value if isinstance(value, int) else pl.multiple_of(value, step)


class Links:
    def __init__(self, dp, space):
        self.dp = dp
        self.space = space
        self.sent = []

    def copy(self, src, dst, ssem, rsem, dp, space):
        return pltpu.make_async_remote_copy(
            src_ref=src, dst_ref=dst, send_sem=ssem, recv_sem=rsem, device_id=(dp, space), device_id_type=MESH
        )

    def send(self, src, dst, ssem, rsem, dp=None, space=None):
        c = self.copy(src, dst, ssem, rsem, self.dp if dp is None else dp, self.space if space is None else space)
        c.start()
        self.sent.append(c)

    def arrived(self, ref, rsem):
        self.copy(ref, ref, rsem, rsem, self.dp, self.space).wait_recv()

    def flush(self):
        for c in self.sent:
            c.wait_send()


def shifted(block, d, rows, sign):
    lanes = block.shape[1]
    v = block.reshape(rows, 48, lanes)
    col = lax.broadcasted_iota(jnp.int32, (rows, 48, lanes), 1)
    if sign < 0:
        v = jnp.where(col >= d, pltpu.roll(v, d, 1), 0.0)
    else:
        v = jnp.where(col < 48 - d, pltpu.roll(v, 48 - d, 1), 0.0)
    return v.reshape(rows * 48, lanes)


PIECES = ((0, 0, 2, 96), (0, 2, 3, 48), (1, 0, 2, 96), (1, 2, 3, 48), (2, 0, 2, 96), (2, 2, 3, 48), (3, 0, 1, 48))
HALVES = tuple(piece[3] for piece in PIECES)
CUT = 80
SMALL_BLOCK = 288


def aspp_kernel(
    maps_in, w_in, w_point_in, w_pool_in, bias_in, w_proj_in, bias_proj_in, cot_in,
    head_to, d_to, d3_to, maps_out,
    maps, w, w_point, w_pool, bias, w_proj, bias_proj, cot, head_out, d, d3,
    x, c, core_out, core_in, acc, sa, sb, ra, rb, s2p, s2m, r2p, r2m, sz, rz, zs, zin, wp, slopes, acts,
    gp, g3, xt, dw, dw3, own, gpo, gpi, gps, gpr, note, note_in, note_sum, notes, gx,
    in_s, out_s, x_s, x_r, wp_s, wp_r, wf_s, wf_r, rs_s, rs_r,
    ag_s, ag_r, ar_s, ar_r, gp_s, gp_r, note_s, note_r, gx_s, gx_r, *pieces,
):
    u1s, u1r, u2s, u2r, es, zr, zt = [pieces[7 * i : 7 * i + 7] for i in range(7)]
    dp = lax.axis_index("dp")
    s = lax.axis_index("space")
    core = s % 2
    chip = s // 2
    cx = chip % 4
    cz = chip // 4
    xp = (cx + 1) % 4
    xm = (cx + 3) % 4
    x2 = (cx + 2) % 4

    def at(z, col, half):
        return (z * 4 + col) * 2 + half

    right = at(cz, xp, core)
    left = at(cz, xm, core)
    other_z = at(1 - cz, cx, core)
    sibling = at(cz, cx, 1 - core)
    y = dp % 4
    hz = dp // 4
    yp = (y + 1) % 4
    ym = (y + 3) % 4
    y2 = (y + 2) % 4
    up = hz * 4 + yp
    down = hz * 4 + ym
    links = Links(dp, s)

    loads = [
        pltpu.make_async_copy(source, target, in_s.at[i])
        for i, (source, target) in enumerate((
            (maps_in, maps), (w_proj_in, w_proj), (w_point_in, w_point), (w_pool_in, w_pool), (bias_in, bias),
            (bias_proj_in, bias_proj), (cot_in, cot), (w_in, w),
        ))
    ]
    for load in loads:
        load.start()
    barrier = pltpu.get_barrier_semaphore()

    @pl.loop(1, 16)
    def _(o):
        pl.semaphore_signal(barrier, inc=1, device_id=(dp, (s + o) % 16), device_id_type=MESH)

    pl.semaphore_signal(barrier, inc=1, device_id=(up, s), device_id_type=MESH)
    pl.semaphore_signal(barrier, inc=1, device_id=(down, s), device_id_type=MESH)
    for o in range(1, 4):
        pl.semaphore_signal(barrier, inc=1, device_id=(((hz + o) % 4) * 4 + y, s), device_id_type=MESH)
    pl.semaphore_wait(barrier, 20)

    def map_copy(o):
        t = (s + o) % 16
        return links.copy(
            maps.at[:, pl.ds(aligned(t * 128, 128), 128)], x.at[pl.ds(aligned(s * ROWS), ROWS)],
            x_s.at[o], x_r.at[o], dp, t,
        )

    loads[0].wait()

    @pl.loop(1, 16)
    def _(o):
        map_copy(o).start()

    for load in loads[1:7]:
        load.wait()

    x[pl.ds(aligned(s * ROWS), ROWS)] = maps[:, pl.ds(aligned(s * 128, 128), 128)]
    wp[:, pl.ds(aligned(s * 16), 16)] = w_proj[...]
    for k in range(3):
        c[k, 0:PAD] = jnp.zeros((PAD, 384), bf16)
        c[k, PAD + PIX : PAD + PIX + PAD] = jnp.zeros((PAD, 384), bf16)
        gp[k, 0:PAD] = jnp.zeros((PAD, 256), bf16)
        gp[k, PAD + PIX : PAD + PIX + PAD] = jnp.zeros((PAD, 256), bf16)

    def build(o, total):
        t = (s + 16 - o) % 16
        base = aligned(t * ROWS)
        raw = x[pl.ds(base, ROWS)]
        v = raw.astype(f32)
        for k, d in enumerate(dilations):
            lo = shifted(v, d, 3, -1).astype(bf16)
            hi = shifted(v, d, 3, 1).astype(bf16)
            c[k, pl.ds(aligned(PAD + base), ROWS)] = jnp.concatenate([lo, raw, hi], axis=1)
        return total + jnp.sum(v.reshape(18, 8, 128), axis=0)

    total = build(0, jnp.zeros((8, 128), f32))

    def build_remote(o, total):
        t = (s + 16 - o) % 16
        links.arrived(x.at[pl.ds(aligned(t * ROWS), ROWS)], x_r.at[o])
        return build(o, total)

    total = lax.fori_loop(1, 16, build_remote, total)

    def proj_part(t):
        return wp.at[:, pl.ds(aligned(t * 16), 16)]

    def proj_copy(o):
        t = ((chip + o) % 8) * 2 + core
        return links.copy(proj_part(s), proj_part(s), wp_s.at[o], wp_r.at[o], dp, t)

    def proj_forward(o):
        t = ((chip + 8 - o) % 8) * 2 + core
        return links.copy(proj_part(t), proj_part(t), wf_s.at[o], wf_r.at[o], dp, sibling)

    @pl.loop(1, 8)
    def _(o):
        proj_copy(o).start()

    proj_forward(0).start()

    def note_first(n):
        links.send(note.at[n], note_in.at[n], note_s.at[n, 8], note_r.at[n, 8], space=sibling)

    def note_copy(n, o):
        t = ((chip + o) % 8) * 2 + core
        return links.copy(note_sum.at[n], notes.at[n, chip], note_s.at[n, o], note_r.at[n, o], dp, t)

    def note_second(n):
        links.arrived(note_in.at[n], note_r.at[n, 8])
        note_sum[n] = note[n] + note_in[n]
        notes[n, pl.ds(chip, 1)] = note_sum[n][None]

        @pl.loop(1, 8)
        def _(o):
            note_copy(n, o).start()

    def note_total(n):
        @pl.loop(1, 8)
        def _(o):
            links.arrived(notes.at[n, (chip + 8 - o) % 8], note_r.at[n, o])

        return lax.fori_loop(0, 8, lambda i, v: v + notes[n, i], jnp.zeros((8, 256), f32))

    def respond(k, lo, hi):
        @pl.loop(lo, hi)
        def _(i):
            base = aligned(i * BLOCK)
            if k < 3:
                d = dilations[k] * 48
                lhs = jnp.concatenate(
                    [c[k, pl.ds(aligned(PAD + base + (a - 1) * d), BLOCK)] for a in range(3)], axis=1
                )
                p = dot(lhs, w[k])
            else:
                p = dot(c[0, pl.ds(aligned(PAD + base), BLOCK), 128:256], w_point[...])
            p = p.reshape(2, 2, ROWS, 256)
            first = core == 0
            acc[k, pl.ds(i * 2, 2)] = jnp.where(first, p[:, 0], p[:, 1])
            core_out[k, pl.ds(i * 2, 2)] = jnp.where(first, p[:, 1], p[:, 0]).astype(bf16)

        if hi == PIX // BLOCK:
            links.send(core_out.at[k], core_in.at[k], rs_s.at[k, 0], rs_r.at[k, 0], space=sibling)

    def step1(k):
        links.arrived(core_in.at[k], rs_r.at[k, 0])

        @pl.loop(0, 8)
        def _(j):
            acc[k, j] = acc[k, j] + core_in[k, j].astype(f32)

        sa[k] = acc[k, x2].astype(bf16)
        links.send(sa.at[k], ra.at[k], rs_s.at[k, 1], rs_r.at[k, 1], space=right)
        sb[k] = acc[k, 4 + x2].astype(bf16)
        links.send(sb.at[k], rb.at[k], rs_s.at[k, 2], rs_r.at[k, 2], space=left)

    def cross1(k):
        links.arrived(core_in.at[k], rs_r.at[k, 0])

        @pl.loop(0, 8)
        def _(j):
            acc[k, j] = acc[k, j] + core_in[k, j].astype(f32)

        @pl.loop(0, 4)
        def _(j):
            zs[j] = acc[k, (1 - cz) * 4 + j].astype(bf16)

        links.send(zs, zin, rs_s.at[k, 1], rs_r.at[k, 1], space=other_z)

    def cross2(k):
        links.arrived(zin, rs_r.at[k, 1])

        @pl.loop(0, 4)
        def _(j):
            acc[k, cz * 4 + j] = acc[k, cz * 4 + j] + zin[j].astype(f32)

        sa[k] = acc[k, cz * 4 + x2].astype(bf16)
        upper, lower = pl.ds(0, CUT), pl.ds(CUT, ROWS - CUT)
        links.send(sa.at[k, upper], ra.at[k, upper], rs_s.at[k, 2], rs_r.at[k, 2], space=right)
        links.send(sa.at[k, lower], ra.at[k, lower], rs_s.at[k, 3], rs_r.at[k, 3], space=left)

    def cross3(k):
        links.arrived(ra.at[k, pl.ds(0, CUT)], rs_r.at[k, 2])
        s2p[k, 0, 0:CUT] = (acc[k, cz * 4 + xp, 0:CUT] + ra[k, 0:CUT].astype(f32)).astype(bf16)
        s2p[k, 0, CUT:ROWS] = acc[k, cz * 4 + xp, CUT:ROWS].astype(bf16)
        links.send(s2p.at[k, 0], r2p.at[k, 0], rs_s.at[k, 4], rs_r.at[k, 4], space=right)
        links.arrived(ra.at[k, pl.ds(CUT, ROWS - CUT)], rs_r.at[k, 3])
        s2m[k, 0, 0:CUT] = acc[k, cz * 4 + xm, 0:CUT].astype(bf16)
        s2m[k, 0, CUT:ROWS] = (acc[k, cz * 4 + xm, CUT:ROWS] + ra[k, CUT:ROWS].astype(f32)).astype(bf16)
        links.send(s2m.at[k, 0], r2m.at[k, 0], rs_s.at[k, 5], rs_r.at[k, 5], space=left)

    def cross4(k):
        links.arrived(r2p.at[k, 0], rs_r.at[k, 4])
        links.arrived(r2m.at[k, 0], rs_r.at[k, 5])
        return acc[k, cz * 4 + cx] + (r2p[k, 0].astype(f32) + r2m[k, 0].astype(f32))

    def step2(k):
        links.arrived(ra.at[k], rs_r.at[k, 1])
        s2p[k, 0] = (acc[k, xp] + ra[k].astype(f32)).astype(bf16)
        s2p[k, 1] = acc[k, 4 + xp].astype(bf16)
        links.send(s2p.at[k], r2p.at[k], rs_s.at[k, 3], rs_r.at[k, 3], space=right)
        links.arrived(rb.at[k], rs_r.at[k, 2])
        s2m[k, 0] = acc[k, xm].astype(bf16)
        s2m[k, 1] = (acc[k, 4 + xm] + rb[k].astype(f32)).astype(bf16)
        links.send(s2m.at[k], r2m.at[k], rs_s.at[k, 4], rs_r.at[k, 4], space=left)

    def step3(k):
        links.arrived(r2p.at[k], rs_r.at[k, 3])
        links.arrived(r2m.at[k], rs_r.at[k, 4])
        for z in range(2):
            acc[k, z * 4 + cx] = acc[k, z * 4 + cx] + (r2p[k, z].astype(f32) + r2m[k, z].astype(f32))
        sz[k] = acc[k, (1 - cz) * 4 + cx].astype(bf16)
        links.send(sz.at[k], rz.at[k], rs_s.at[k, 5], rs_r.at[k, 5], space=other_z)

    def step4(k):
        links.arrived(rz.at[k], rs_r.at[k, 5])
        return acc[k, cz * 4 + cx] + rz[k].astype(f32)

    def turn(lo, hi):
        @pl.loop(lo, hi)
        def _(i):
            st = aligned(i * 384, 128)
            v = x[pl.ds(st, 384)].astype(f32)
            mid = jnp.transpose(v).astype(bf16)
            for k, d in enumerate(dilations):
                xt[k, 0:128, pl.ds(st, 384)] = jnp.transpose(shifted(v, d, 8, -1)).astype(bf16)
                xt[k, 128:256, pl.ds(st, 384)] = mid
                xt[k, 256:384, pl.ds(st, 384)] = jnp.transpose(shifted(v, d, 8, 1)).astype(bf16)

    respond(3, 0, 4)

    pooled = (jnp.sum(total, axis=0, keepdims=True) / PIX).astype(bf16)
    pooled = jnp.broadcast_to(pooled, (16, 128))
    pool_part = dot(pooled, w_pool[...])[0:8]
    note[0] = jnp.zeros((8, 256), f32)
    for i in range(16):
        note[0, 1:6, 16 * i : 16 * i + 16] = bias[...]
    row = lax.broadcasted_iota(jnp.int32, (8, 256), 0)
    lane = lax.broadcasted_iota(jnp.int32, (8, 256), 1)
    mine = (lane >= s * 16) & (lane < s * 16 + 16)
    note[0] = jnp.where(row == 0, pool_part, jnp.where(mine, note[0], 0.0))
    note_first(0)

    loads[7].wait()
    respond(0, 0, 2)
    step1(3)
    note_second(0)
    respond(0, 2, 4)
    respond(1, 0, 2)
    step1(0)
    step2(3)
    respond(1, 2, 4)

    @pl.loop(1, 8)
    def _(o):
        links.arrived(proj_part(((chip + 8 - o) % 8) * 2 + core), wp_r.at[o])
        proj_forward(o).start()

    respond(2, 0, 2)
    cross1(1)
    step2(0)
    step3(3)
    respond(2, 2, 4)
    turn(0, 2)
    step1(2)
    turn(2, 4)
    cross2(1)
    step3(0)
    step2(2)

    @pl.loop(0, 8)
    def _(o):
        links.arrived(proj_part(((chip + 8 - o) % 8) * 2 + 1 - core), wf_r.at[o])

    head_note = note_total(0)
    pool_pre = head_note[0:1] + head_note[5:6]
    pool_act = jnp.broadcast_to(jax.nn.silu(pool_pre).astype(bf16).astype(f32), (ROWS, 256)).astype(bf16)

    def absorb(k):
        pre = (cross4(k) if k == 1 else step4(k)) + head_note[1 + k : 2 + k]
        sigma = jax.nn.sigmoid(pre)
        slopes[k] = sigma * (1.0 + pre * (1.0 - sigma))
        act = (pre * sigma).astype(bf16)
        acts[k] = act
        return dot(act, wp[k])

    head = bias_proj[...] + dot(pool_act, wp[4])
    head = head + absorb(3)
    turn(4, 6)
    cross3(1)
    step3(2)
    head = head + absorb(0)
    head = head + absorb(1)
    head = head + absorb(2)
    sigma = jax.nn.sigmoid(head)
    grad_f = cot[...].astype(f32) * (sigma * (1.0 + head * (1.0 - sigma)))
    grad = grad_f.astype(bf16)

    def block(k, n):
        if k < 3:
            return gp.at[k, pl.ds(aligned(PAD + n * ROWS), ROWS)]
        return g3.at[pl.ds(aligned(n * ROWS), ROWS)]

    def pass_on(k, n, slot, to):
        b = block(k, n)
        links.send(b, b, ag_s.at[k, slot], ag_r.at[k, n], space=to)

    def have(k, n):
        links.arrived(block(k, n), ag_r.at[k, n])

    def own_block(k):
        g = (dot_nt(grad, wp[k]) * slopes[k]).astype(bf16)
        if k < 3:
            gp[k, pl.ds(aligned(PAD + s * ROWS), ROWS)] = g
        else:
            g3[pl.ds(aligned(s * ROWS), ROWS)] = g
        pass_on(k, s, 0, other_z)
        pass_on(k, s, 1, right)
        pass_on(k, s, 2, left)
        pass_on(k, s, 3, sibling)
        note[1, k : k + 1] = jnp.sum(g.astype(f32), axis=0, keepdims=True)

    def head_store():
        head_out[...] = (head * sigma).astype(bf16)
        own_head().start()

    def gather1(k):
        n = at(1 - cz, cx, core)
        have(k, n)
        pass_on(k, n, 4, right)
        pass_on(k, n, 5, left)
        pass_on(k, n, 6, sibling)

    def gather2(k):
        n = at(0, xm, core)
        have(k, n)
        pass_on(k, n, 7, right)
        pass_on(k, n, 8, sibling)
        n = at(1, xp, core)
        have(k, n)
        pass_on(k, n, 9, left)
        pass_on(k, n, 10, sibling)
        n = at(1, xm, core)
        have(k, n)
        pass_on(k, n, 11, sibling)
        n = at(0, xp, core)
        have(k, n)
        pass_on(k, n, 12, sibling)

    def gather3(k):
        for z in range(2):
            n = at(z, x2, core)
            have(k, n)
            pass_on(k, n, 13 + z, sibling)

    def gather4(k):
        for z in range(2):
            for col in (cx, xp, xm, x2):
                have(k, at(z, col, 1 - core))

    def proj_grad():
        for k in range(5):
            act = acts[k] if k < 4 else pool_act
            g = lax.dot_general(act, grad, TN, preferred_element_type=f32).astype(bf16)
            g = g.reshape(8, 2, 16, 256)
            gpo[0, k] = g[:, 0]
            gpo[1, k] = g[:, 1]
        links.send(gpo.at[1 - core], gpi, gp_s.at[0], gp_r.at[0], space=sibling)

    def note_start():
        note[1, 4:5] = jnp.sum(dot_nt(grad, wp[4]), axis=0, keepdims=True)
        note[1, 5:6] = jnp.sum(grad.astype(f32), axis=0, keepdims=True)
        note[1, 6:8] = jnp.zeros((2, 256), f32)
        note_first(1)

    def weight_grad(p):
        k, first, last, _ = PIECES[p]
        d = 48 * dilations[k]
        for a, (lo, hi) in enumerate(
            ((0, -((d - PIX) // 128) * 128), (0, PIX), (d // 128 * 128, PIX))
        ):
            if first <= a < last:
                g0 = PAD + lo - (a - 1) * d
                dw[k, 384 * a : 384 * (a + 1)] = dot(xt[k, :, lo:hi], gp[k, g0 : g0 + hi - lo])

    def summed(p, start, size):
        k, first, _, _ = PIECES[p]
        if k == 3:
            return dw3[pl.ds(aligned(start), size)]
        return dw[k, pl.ds(aligned(384 * first + start), size)]

    def result(p, start, size):
        k, first, _, _ = PIECES[p]
        if k == 3:
            return d3.at[pl.ds(aligned(start), size)]
        return d.at[k, pl.ds(aligned(384 * first + start), size)]

    def sum1(k):
        h = HALVES[k]
        u1s[k][0] = summed(k, y2 * 2 * h, h).astype(bf16)
        links.send(u1s[k].at[0], u1r[k].at[0], ar_s.at[k, 0], ar_r.at[k, 0], dp=up)
        u1s[k][1] = summed(k, y2 * 2 * h + h, h).astype(bf16)
        links.send(u1s[k].at[1], u1r[k].at[1], ar_s.at[k, 1], ar_r.at[k, 1], dp=down)

    def sum2(k):
        h = HALVES[k]
        links.arrived(u1r[k].at[0], ar_r.at[k, 0])
        u2s[k][0, 0] = (summed(k, yp * 2 * h, h) + u1r[k][0].astype(f32)).astype(bf16)
        u2s[k][0, 1] = summed(k, yp * 2 * h + h, h).astype(bf16)
        links.send(u2s[k].at[0], u2r[k].at[0], ar_s.at[k, 2], ar_r.at[k, 2], dp=up)
        links.arrived(u1r[k].at[1], ar_r.at[k, 1])
        u2s[k][1, 0] = summed(k, ym * 2 * h, h).astype(bf16)
        u2s[k][1, 1] = (summed(k, ym * 2 * h + h, h) + u1r[k][1].astype(f32)).astype(bf16)
        links.send(u2s[k].at[1], u2r[k].at[1], ar_s.at[k, 3], ar_r.at[k, 3], dp=down)

    def sum3(k):
        h = HALVES[k]
        links.arrived(u2r[k].at[0], ar_r.at[k, 2])
        links.arrived(u2r[k].at[1], ar_r.at[k, 3])
        for half in range(2):
            v = summed(k, y * 2 * h + half * h, h) + (
                u2r[k][0, half].astype(f32) + u2r[k][1, half].astype(f32)
            )
            for lanes in range(2):
                quarter = v[:, 128 * lanes : 128 * (lanes + 1)]
                own[k, 2 * half + lanes, 0:h] = quarter
                es[k][2 * half + lanes] = quarter.astype(bf16)
        for o in range(1, 4):
            q = (hz + o) % 4
            links.send(es[k].at[q], zr[k].at[o - 1], ar_s.at[k, 3 + o], ar_r.at[k, 3 + o], dp=q * 4 + y)

    def sum4(k):
        h = HALVES[k]
        v = own[k, hz, 0:h]
        for o in range(1, 4):
            links.arrived(zr[k].at[o - 1], ar_r.at[k, 3 + o])
            v = v + zr[k][o - 1].astype(f32)
        zt[k][hz] = v.astype(bf16)
        for o in range(1, 4):
            q = (hz + o) % 4
            links.send(zt[k].at[hz], zt[k].at[hz], ar_s.at[k, 6 + o], ar_r.at[k, 6 + o], dp=q * 4 + y)

    def chunk(k, n):
        h = HALVES[k]
        return result(k, n * 2 * h, 2 * h)

    def half_chunk(k, n, half):
        h = HALVES[k]
        return result(k, n * 2 * h + half * h, h)

    def sum5(k):
        h = HALVES[k]
        for o in range(1, 4):
            links.arrived(zt[k].at[(hz + 4 - o) % 4], ar_r.at[k, 6 + o])
        for half in range(2):
            result(k, y * 2 * h + half * h, h)[...] = jnp.concatenate(
                [zt[k][2 * half], zt[k][2 * half + 1]], axis=1
            )
        share = chunk(k, y)
        links.send(share, share, ar_s.at[k, 10], ar_r.at[k, 10], dp=up)
        links.send(share, share, ar_s.at[k, 11], ar_r.at[k, 11], dp=down)

    def sum6(k):
        links.arrived(chunk(k, ym), ar_r.at[k, 10])
        b = half_chunk(k, ym, 0)
        links.send(b, b, ar_s.at[k, 12], ar_r.at[k, 12], dp=up)
        links.arrived(chunk(k, yp), ar_r.at[k, 11])
        b = half_chunk(k, yp, 1)
        links.send(b, b, ar_s.at[k, 13], ar_r.at[k, 13], dp=down)

    def store(p):
        k, first, last, _ = PIECES[p]
        if k == 3:
            return pltpu.make_async_copy(d3, d3_to, out_s.at[p])
        rows = pl.ds(384 * first, 384 * (last - first))
        return pltpu.make_async_copy(d.at[k, rows], d_to.at[k, rows], out_s.at[p])

    def sum7(k):
        links.arrived(half_chunk(k, y2, 0), ar_r.at[k, 12])
        links.arrived(half_chunk(k, y2, 1), ar_r.at[k, 13])
        store(k).start()

    def proj_grad_copy(o):
        j = (chip + o) % 8
        return links.copy(gps.at[:, j], gpr.at[chip], gp_s.at[o], gp_r.at[o], dp, j * 2 + core)

    def proj_grad_share():
        links.arrived(gpi, gp_r.at[0])
        gps[...] = (gpo[core].astype(f32) + gpi[...].astype(f32)).astype(bf16)

        @pl.loop(1, 8)
        def _(o):
            proj_grad_copy(o).start()

    def small_grads():
        dw3[0:128] = dot(xt[0, 128:256, :], g3[...])
        totals = note_total(1)
        pool_grad = (silu_slope(pool_pre) * totals[4:5]).astype(bf16)
        pool_row = pool_grad.astype(f32)
        column = jnp.transpose(jnp.broadcast_to(pooled[0:1].astype(f32), (128, 128)))
        dw3[128:256] = jnp.concatenate([column, column], axis=1) * pool_row

        @pl.loop(1, 8)
        def _(o):
            links.arrived(gpr.at[(chip + 8 - o) % 8], gp_r.at[o])

        gpr[pl.ds(chip, 1)] = gps[:, pl.ds(chip, 1)].reshape(1, 5, 16, 256)
        dw3[256:336] = lax.fori_loop(
            0, 8, lambda i, v: v + gpr[i].astype(f32).reshape(80, 256), jnp.zeros((80, 256), f32)
        )
        dw3[336:384] = jnp.zeros((48, 256), f32)
        dw3[336:340] = totals[0:4]
        dw3[340:341] = pool_row
        dw3[341:342] = totals[5:6]
        return dot_nt(jnp.broadcast_to(pool_row, (16, 256)).astype(bf16), w_pool[...])[0:1] / PIX

    def input_grad(i):
        size = SMALL_BLOCK
        st = i * size
        total = dot_nt(g3[st : st + size], w_point[...]) + back
        for k in range(3):
            d = 48 * dilations[k]
            sides = 0.0
            for a in range(3):
                g0 = PAD + st - (a - 1) * d
                g = gp[k, g0 : g0 + size]
                tap = 384 * a
                ends = jnp.concatenate([w[k, tap : tap + 128], w[k, tap + 256 : tap + 384]], axis=0)
                sides = sides + dot_nt(g, ends)
                total = total + dot_nt(g, w[k, tap + 128 : tap + 256])
            total = total + shifted(sides[:, 0:128], dilations[k], size // 48, 1)
            total = total + shifted(sides[:, 128:256], dilations[k], size // 48, -1)
        gx[st : st + size] = total.astype(bf16)
        for j in range(size // ROWS):
            n = i * (size // ROWS) + j

            @pl.when(s != n)
            def _():
                gx_copy(n).start()

    def gx_copy(n):
        return links.copy(
            gx.at[pl.ds(n * ROWS, ROWS)], maps_out.at[:, pl.ds(aligned(s * 128, 128), 128)],
            gx_s.at[n], gx_r.at[s], dp, n,
        )

    def own_maps():
        return pltpu.make_async_copy(
            gx.at[pl.ds(aligned(s * ROWS), ROWS)], maps_out.at[:, pl.ds(aligned(s * 128, 128), 128)], out_s.at[7]
        )

    def own_head():
        return pltpu.make_async_copy(head_out, head_to, out_s.at[8])

    def collect():
        own_maps().start()

        @pl.loop(1, 16)
        def _(o):
            t = (s + o) % 16
            links.arrived(maps_out.at[:, pl.ds(aligned(t * 128, 128), 128)], gx_r.at[t])

    own_block(2)
    own_block(0)
    own_block(1)
    gather1(2)
    proj_grad()
    head_store()
    gather1(0)
    own_block(3)
    gather2(2)
    note_start()
    gather1(1)
    gather2(0)
    gather3(2)
    gather1(3)
    note_second(1)
    gather4(2)
    weight_grad(5)
    gather2(1)
    sum1(5)
    gather3(0)
    weight_grad(4)
    sum1(4)
    gather4(0)
    weight_grad(0)
    sum1(0)
    gather2(3)
    sum2(5)
    gather3(1)
    proj_grad_share()
    sum2(4)
    weight_grad(1)
    sum1(1)
    gather4(1)
    weight_grad(2)
    sum2(0)
    sum3(5)
    gather3(3)
    weight_grad(3)
    sum1(3)
    sum1(2)
    sum3(4)
    gather4(3)
    sum2(1)
    back = small_grads()
    sum1(6)
    sum4(5)
    sum2(3)
    sum3(0)
    sum2(2)
    sum4(4)
    sum5(5)
    sum3(1)
    sum3(3)
    sum2(6)
    sum3(2)
    sum4(0)
    input_grad(0)
    sum5(4)
    sum3(6)
    sum4(3)
    sum4(2)
    sum6(4)
    sum5(0)
    sum4(1)
    sum6(5)
    sum4(6)
    input_grad(1)
    sum5(3)
    input_grad(2)
    sum5(2)
    input_grad(3)
    input_grad(4)
    sum5(6)
    sum5(1)
    input_grad(5)
    sum7(4)
    sum6(0)
    sum6(3)
    input_grad(6)
    sum6(2)
    input_grad(7)
    sum6(6)
    sum6(1)
    sum7(3)
    collect()
    sum7(5)
    sum7(0)
    sum7(6)
    sum7(2)
    sum7(1)

    @pl.loop(1, 16)
    def _(o):
        t = (s + o) % 16
        map_copy(o).wait_send()
        links.copy(
            gx.at[pl.ds(0, ROWS)], gx.at[pl.ds(0, ROWS)], gx_s.at[t], gx_s.at[t], dp, t
        ).wait_send()

    proj_forward(0).wait_send()

    @pl.loop(1, 8)
    def _(o):
        proj_copy(o).wait_send()
        proj_forward(o).wait_send()
        note_copy(0, o).wait_send()
        note_copy(1, o).wait_send()
        proj_grad_copy(o).wait_send()

    own_maps().wait()
    own_head().wait()
    for p in range(7):
        store(p).wait()
    links.flush()


def finish_kernel(
    head_in, d_in, d3_in, maps_in, head_out, maps_out, atrous, point, pool, bias, proj, proj_bias,
    d, d3, wide, wide3, maps, head, in_s, out_s,
):
    s = lax.axis_index("space")
    loads = [pltpu.make_async_copy(d3_in, d3, in_s.at[6])]
    loads += [pltpu.make_async_copy(half(d_in, i), half(d, i), in_s.at[i]) for i in range(6)]
    loads += [pltpu.make_async_copy(maps_in, maps, in_s.at[7]), pltpu.make_async_copy(head_in, head, in_s.at[8])]
    for copy in loads:
        copy.start()
    loads[0].wait()
    wide3[...] = d3[0:336].astype(f32)
    rows = d3[336:352].astype(f32)
    picked = jnp.zeros((5, 16), f32)
    for i in range(16):
        picked = jnp.where(s == i, rows[0:5, 16 * i : 16 * i + 16], picked)
    bias[...] = picked
    proj_bias[...] = rows[5:6]
    stores = [
        pltpu.make_async_copy(wide3.at[pl.ds(0, 128)], point, out_s.at[8]),
        pltpu.make_async_copy(wide3.at[pl.ds(128, 128)], pool, out_s.at[9]),
        pltpu.make_async_copy(wide3.at[pl.ds(256, 80)], proj, out_s.at[10]),
    ]
    for copy in stores:
        copy.start()
    for i in range(6):
        loads[1 + i].wait()
        k, first = i // 2, 576 * (i % 2)
        wide[k, first : first + 576] = d[k, first : first + 576].astype(f32)
        copy = pltpu.make_async_copy(half(wide, i), half(atrous, i), out_s.at[i])
        copy.start()
        stores.append(copy)
    loads[7].wait()
    loads[8].wait()
    through = [
        pltpu.make_async_copy(maps, maps_out, out_s.at[6]), pltpu.make_async_copy(head, head_out, out_s.at[7]),
    ]
    for copy in through:
        copy.start()
    for copy in stores + through:
        copy.wait()


def half(array, i):
    return array.at[i // 2, pl.ds(576 * (i % 2), 576)]


def dma(*shape):
    return pltpu.SemaphoreType.DMA(shape)


def vm(dtype, *shape):
    return pltpu.VMEM(shape, dtype)


def body(feature_maps, w_atrous, w_point, w_pool, bias_branch, w_proj, bias_proj, cotangent):
    hbm = pl.BlockSpec(memory_space=pl.ANY)
    vmem = pl.BlockSpec(memory_space=pltpu.VMEM)
    shape = jax.ShapeDtypeStruct
    results = pl.pallas_call(
        aspp_kernel,
        out_shape=(
            shape((ROWS, 256), bf16), shape((3, 1152, 256), bf16), shape((384, 256), bf16),
            shape((ROWS, 2048), bf16),
        ),
        in_specs=[hbm] * 8,
        out_specs=[hbm] * 4,
        scratch_shapes=[
            vm(bf16, ROWS, 2048), vm(bf16, 3, 1152, 256), vm(bf16, 128, 256), vm(bf16, 128, 256), vm(f32, 5, 16),
            vm(bf16, 5, 16, 256), vm(f32, 1, 256), vm(bf16, ROWS, 256),
            vm(bf16, ROWS, 256), vm(bf16, 3, 1152, 256), vm(bf16, 384, 256),
            vm(bf16, PIX, 128), vm(bf16, 3, PIX + 2 * PAD, 384),
            vm(bf16, 4, 8, ROWS, 256), vm(bf16, 4, 8, ROWS, 256), vm(f32, 4, 8, ROWS, 256),
            vm(bf16, 4, ROWS, 256), vm(bf16, 4, ROWS, 256), vm(bf16, 4, ROWS, 256), vm(bf16, 4, ROWS, 256),
            vm(bf16, 4, 2, ROWS, 256), vm(bf16, 4, 2, ROWS, 256),
            vm(bf16, 4, 2, ROWS, 256), vm(bf16, 4, 2, ROWS, 256),
            vm(bf16, 4, ROWS, 256), vm(bf16, 4, ROWS, 256), vm(bf16, 4, ROWS, 256), vm(bf16, 4, ROWS, 256),
            vm(bf16, 5, 256, 256), vm(f32, 4, ROWS, 256), vm(bf16, 4, ROWS, 256),
            vm(bf16, 3, PIX + 2 * PAD, 256), vm(bf16, PIX, 256), vm(bf16, 3, 384, PIX),
            vm(f32, 3, 1152, 256), vm(f32, 384, 256), vm(f32, 7, 4, 96, 128),
            vm(bf16, 2, 5, 8, 16, 256), vm(bf16, 5, 8, 16, 256), vm(bf16, 5, 8, 16, 256),
            vm(bf16, 8, 5, 16, 256),
            vm(f32, 2, 8, 256), vm(f32, 2, 8, 256), vm(f32, 2, 8, 256), vm(f32, 2, 8, 8, 256),
            vm(bf16, PIX, 128),
            dma(8), dma(9), dma(16), dma(16), dma(8), dma(8), dma(8), dma(8), dma(4, 6), dma(4, 6),
            dma(4, 15), dma(4, 16), dma(7, 14), dma(7, 14),
            dma(8), dma(8), dma(2, 9), dma(2, 9), dma(16), dma(16),
            *[vm(bf16, 2, h, 256) for h in HALVES], *[vm(bf16, 2, h, 256) for h in HALVES],
            *[vm(bf16, 2, 2, h, 256) for h in HALVES], *[vm(bf16, 2, 2, h, 256) for h in HALVES],
            *[vm(bf16, 4, h, 128) for h in HALVES], *[vm(bf16, 3, h, 128) for h in HALVES],
            *[vm(bf16, 4, h, 128) for h in HALVES],
        ],
        compiler_params=pltpu.CompilerParams(
            collective_id=0, has_side_effects=True, vmem_limit_bytes=VMEM_LIMIT
        ),
        name="aspp",
    )(
        feature_maps.reshape(ROWS, 2048), w_atrous.reshape(3, 1152, 256), w_point, w_pool, bias_branch,
        w_proj, bias_proj.reshape(1, 256), cotangent.reshape(ROWS, 256),
    )
    head_out, grad_maps, atrous, point, pool, bias, proj, proj_bias = pl.pallas_call(
        finish_kernel,
        out_shape=(
            shape((ROWS, 256), bf16), shape((ROWS, 2048), bf16), shape((3, 1152, 256), f32),
            shape((128, 256), f32), shape((128, 256), f32), shape((5, 16), f32), shape((80, 256), f32),
            shape((1, 256), f32),
        ),
        in_specs=[hbm] * 4,
        out_specs=[hbm] * 5 + [vmem, hbm, vmem],
        scratch_shapes=[
            vm(bf16, 3, 1152, 256), vm(bf16, 384, 256), vm(f32, 3, 1152, 256), vm(f32, 336, 256),
            vm(bf16, ROWS, 2048), vm(bf16, ROWS, 256), dma(9), dma(11),
        ],
        compiler_params=pltpu.CompilerParams(vmem_limit_bytes=VMEM_LIMIT),
        name="finish",
    )(*results)
    return (
        head_out.reshape(1, 3, 48, 256),
        grad_maps.reshape(1, 3, 48, 2048),
        atrous.reshape(3, 9, 128, 256),
        point,
        pool,
        bias,
        proj.reshape(5, 16, 256),
        proj_bias.reshape(256),
    )


def solution(mesh):
    placed = (
        P("dp", "space", None, None),
        P(None, None, "space", None),
        P("space", None),
        P("space", None),
        P(None, "space"),
        P(None, "space", None),
        P(),
        P("dp", "space", None, None),
    )
    return jax.shard_map(
        body,
        mesh=mesh,
        in_specs=placed,
        out_specs=(
            P("dp", "space", None, None),
            P("dp", "space", None, None),
            P(None, None, "space", None),
            P("space", None),
            P("space", None),
            P(None, "space"),
            P(None, "space", None),
            P(),
        ),
        check_vma=False,
    )
```
